32 devices in a mesh: dp: 16 (over z, x, core), ctx: 2 (over y).
Axes of the slice: x: 2, y: 2, z: 4, core: 2. Of those that a mesh axis runs over, the one named last changes fastest.
Arguments:
- tokens: bfloat16 [32768, 896], P(('dp', 'ctx')), may hold values from -6 to 6
- image_starts: int32 [16, 2], P('dp'), may hold values from 0 to 1792
- attn_gain: bfloat16 [896], P(('dp', 'ctx')), may hold values from 0.5 to 1.5
- query_weight: bfloat16 [896, 896], P(('dp', 'ctx')), may hold values from -0.1875 to 0.1875
- query_bias: bfloat16 [896], P(('dp', 'ctx')), may hold values from -3 to 3
- key_weight: bfloat16 [896, 128], P(('dp', 'ctx')), may hold values from -0.1875 to 0.1875
- key_bias: bfloat16 [128], P(('dp', 'ctx')), may hold values from -3 to 3
- value_weight: bfloat16 [896, 128], P(('dp', 'ctx')), may hold values from -0.1875 to 0.1875
- value_bias: bfloat16 [128], P(('dp', 'ctx')), may hold values from -2 to 2
- out_weight: bfloat16 [896, 896], P(('dp', 'ctx')), may hold values from -1.5 to 1.5
- mlp_gain: bfloat16 [896], P(('dp', 'ctx')), may hold values from 0.5 to 1.5
- gate_weight: bfloat16 [896, 4864], P(('dp', 'ctx')), may hold values from -0.1875 to 0.1875
- up_weight: bfloat16 [896, 4864], P(('dp', 'ctx')), may hold values from -0.1875 to 0.1875
- down_weight: bfloat16 [896, 4864], P(('dp', 'ctx')), may hold values from -0.078125 to 0.078125
- cotangent: bfloat16 [32768, 896], P(('dp', 'ctx')), may hold values from -6 to 6
Outputs:
- output: bfloat16 [32768, 896], P(('dp', 'ctx'))
- tokens_grad: bfloat16 [32768, 896], P(('dp', 'ctx'))
- attn_gain_grad: float32 [896], P(('dp', 'ctx'))
- query_weight_grad: float32 [896, 896], P(('dp', 'ctx'))
- query_bias_grad: float32 [896], P(('dp', 'ctx'))
- key_weight_grad: float32 [896, 128], P(('dp', 'ctx'))
- key_bias_grad: float32 [128], P(('dp', 'ctx'))
- value_weight_grad: float32 [896, 128], P(('dp', 'ctx'))
- value_bias_grad: float32 [128], P(('dp', 'ctx'))
- out_weight_grad: float32 [896, 896], P(('dp', 'ctx'))
- mlp_gain_grad: float32 [896], P(('dp', 'ctx'))
- gate_weight_grad: float32 [896, 4864], P(('dp', 'ctx'))
- up_weight_grad: float32 [896, 4864], P(('dp', 'ctx'))
- down_weight_grad: float32 [896, 4864], P(('dp', 'ctx'))
The draws below stay inside these ranges and needn't reach their ends.
Inputs may be any that keep to these rules, and one draw needn't show every extreme that they name: `image_starts`: row s gives the first positions of the 2 picture pieces of sequence s, each 256 tokens long; pieces may intersect.
All inputs are finite; a program needn't handle non-finite values.
Results may differ from the reference program's by a relative error of at most 0.018.
Values may be sent and summed in bfloat16 or wider, within the bound.
No kernel may reach another device: no remote copies, remote signals or barrier semaphores. Data moves between devices by JAX's collectives and lax.ppermute only.
A program may use at most 320 MiB of HBM per device.

```python
import jax
import jax.numpy as jnp
from jax import lax

D = 896
H = 14
KV = 2
HD = 64
FF = 4864
IMG = 256
NIMG = 2
LENGTH = 2048
SEQS = 16
TOKENS = 32768


def plant(array, rng, least, largest):
    spot = [jax.random.randint(jax.random.fold_in(rng, axis), (), 0, length) for axis, length in enumerate(array.shape)]
    main_axis = array.shape.index(max(array.shape))
    next_to = spot[:main_axis] + [(spot[main_axis] + 1) % array.shape[main_axis]] + spot[main_axis + 1:]
    return array.at[tuple(spot)].set(least).at[tuple(next_to)].set(largest)


def with_spikes(drawn, stream_key, source, target, shards_of, factor):
    owner, partner = [(jnp.arange(drawn.shape[position]) // (drawn.shape[position] // shards_of)).reshape([-1 if axis == position else 1 for axis in range(drawn.ndim)]) for position in (source, target)]
    chosen = jax.random.permutation(stream_key, shards_of)[partner]
    strong = (owner == chosen) | (owner == (partner + shards_of // 2) % shards_of)
    return jnp.where(strong, factor * drawn, drawn)


def steps_of(key, shape, shards, low, high):
    def one(dim, shards_of):
        draws = jax.random.uniform(jax.random.fold_in(jax.random.fold_in(key, 6), dim), (shards_of,), jnp.float32, low / len(shards), high / len(shards))
        return jnp.repeat(jnp.exp(draws), shape[dim] // shards_of).reshape((-1,) + (1,) * (len(shape) - dim - 1))

    level = one(*shards[0])
    for cut in shards[1:]:
        level = level * one(*cut)
    return level


def normal_values(key, dims, scale, most, pieces=(), held_as=jnp.bfloat16):
    entries = jax.random.normal(key, dims, jnp.float32) * scale
    if len(pieces) > 0:
        entries = steps_of(key, dims, pieces, -0.22, 0.18) * entries
    return jnp.clip(entries, min=-most, max=most).astype(held_as)


def heavy_noise(rng, dims, scale, limit, split, heavy, kind=jnp.bfloat16):
    entries = scale * jax.random.normal(rng, dims, jnp.float32)
    if split:
        entries = entries * steps_of(rng, dims, split, -0.22, 0.18)
    return jnp.clip(with_spikes(entries, jax.random.fold_in(rng, 3), *heavy), -limit, limit).astype(kind)


def setup_inputs(seed: int = 0) -> dict:
    splits = jax.random.split(jax.random.key(seed), 16)
    return {
        "tokens": normal_values(splits[0], (TOKENS, D), 1.0, 6.0, ((0, 32),)),
        "image_starts": plant(jax.random.randint(splits[1], (SEQS, NIMG), 0, LENGTH - IMG + 1), jax.random.fold_in(splits[1], 1), 0, LENGTH - IMG).astype(jnp.int32),
        "attn_gain": jnp.clip(1.0 + 0.1 * jax.random.normal(splits[2], (D,), jnp.float32), 0.5, 1.5).astype(jnp.bfloat16),
        "query_weight": normal_values(splits[3], (D, H * HD), D ** -0.5, 0.1875, ((0, 32),)),
        "query_bias": normal_values(splits[4], (H * HD,), 0.5, 3.0, ((0, 32),)),
        "key_weight": normal_values(splits[5], (D, KV * HD), D ** -0.5, 0.1875, ((0, 32),)),
        "key_bias": normal_values(splits[6], (KV * HD,), 0.5, 3.0, ((0, 32),)),
        "value_weight": normal_values(splits[7], (D, KV * HD), D ** -0.5, 0.1875, ((0, 32),)),
        "value_bias": normal_values(splits[8], (KV * HD,), 0.3, 2.0, ((0, 32),)),
        "out_weight": normal_values(splits[9], (D, H * HD), (max(H * HD // 64, 2)) ** -0.5, 1.5, ((0, 32),)),
        "mlp_gain": jnp.clip(1.0 + 0.1 * jax.random.normal(splits[10], (D,), jnp.float32), 0.5, 1.5).astype(jnp.bfloat16),
        "gate_weight": normal_values(splits[11], (D, FF), D ** -0.5, 0.1875, ((0, 32),)),
        "up_weight": normal_values(splits[12], (D, FF), D ** -0.5, 0.1875, ((0, 32),)),
        "down_weight": normal_values(splits[13], (D, FF), FF ** -0.5, 0.078125, ((0, 32),)),
        "cotangent": heavy_noise(splits[14], (TOKENS, D), 1.0, 6.0, ((0, 32),), (0, 1, 32, 2.75)),
    }


eps = 1e-06
rope_base = 1000000.0
neg_fill = -1e+30
highest = lax.Precision.HIGHEST

@jax.custom_vjp
def low(v):
    return lax.optimization_barrier(v.astype(jnp.bfloat16)).astype(jnp.float32)

@jax.custom_vjp
def low_back(v):
    return v

def low_keep(v):
    return (low(v), None)

def low_pass(kept, grad):
    return (grad,)

def back_keep(v):
    return (v, None)

def back_low(kept, grad):
    return (low(grad),)
low.defvjp(low_keep, low_pass)
low_back.defvjp(back_keep, back_low)

def norm_scaled(values, gain):
    return values * lax.rsqrt(lax.optimization_barrier(jnp.mean(values * values, axis=-1, keepdims=True)) + eps) * gain

def rotate(values, positions):
    count = values.shape[0]
    heads = values.shape[1] // HD
    half_dim = HD // 2
    inverse = rope_base ** (-(jnp.arange(half_dim).astype(jnp.float32) * 2.0 / HD))
    angles = positions.astype(jnp.float32)[:, None] * inverse[None, :]
    cosine = jnp.cos(angles)[:, None, :]
    sine_vals = jnp.sin(angles)[:, None, :]
    shaped = values.reshape(count, heads, 2, half_dim)
    first = shaped[:, :, 0]
    second = shaped[:, :, 1]
    turned_a = first * cosine - second * sine_vals
    turned_b = second * cosine + first * sine_vals
    return jnp.stack([turned_a, turned_b], axis=2).reshape(count, heads * HD)

def visible(query_pos, key_pos, starts_row):
    causal = key_pos[None, :] <= query_pos[:, None]
    query_in = (query_pos[:, None] >= starts_row[None, :]) & (query_pos[:, None] < starts_row[None, :] + IMG)
    key_in = (key_pos[:, None] >= starts_row[None, :]) & (key_pos[:, None] < starts_row[None, :] + IMG)
    same_piece = jnp.any(query_in[:, None, :] & key_in[None, :, :], axis=-1)
    return causal | same_piece

def matmul(left, right):
    return jnp.dot(left, right, precision=highest)

def matmul_t(left, right):
    return lax.dot_general(left, right, (((1,), (1,)), ((), ())), precision=highest)

def one_sequence(params, seq_tokens, starts_row):
    gain_attn, query_full, query_shift, key_full, key_shift, value_full, value_shift, out_full, gain_mlp, gate_full, up_full, down_full = params
    seq_len = seq_tokens.shape[0]
    kv_heads = key_full.shape[1] // HD
    query_heads = query_full.shape[1] // HD
    per_group = query_heads // kv_heads
    positions = jnp.arange(seq_len).astype(jnp.int32)
    normed_one = low(norm_scaled(seq_tokens, gain_attn))
    query_pre = low_back(matmul(normed_one, query_full) + query_shift)
    key_pre = low_back(matmul(normed_one, key_full) + key_shift)
    value_in = low(low_back(matmul(normed_one, value_full) + value_shift))
    queries = low(rotate(query_pre, positions)).reshape(seq_len, kv_heads, per_group, HD)
    key_heads = low(rotate(key_pre, positions)).reshape(seq_len, kv_heads, HD)
    value_heads = value_in.reshape(seq_len, kv_heads, HD)
    scores = low_back(jnp.einsum('skgd,tkd->kgst', queries, key_heads, precision=highest))
    allowed = visible(positions, positions, starts_row)
    masked = jnp.where(allowed[None, None], scores * HD ** (-0.5), neg_fill)
    probs = jax.nn.softmax(masked, axis=-1)
    mixed = jnp.einsum('kgst,tkd->skgd', low(probs), value_heads, precision=highest)
    attended = low(low_back(mixed.reshape(seq_len, query_heads * HD)))
    hidden_one = seq_tokens + low_back(matmul_t(attended, out_full))
    normed_two = low(norm_scaled(hidden_one, gain_mlp))
    gate_vals = low_back(matmul(normed_two, gate_full))
    up_vals = low_back(matmul(normed_two, up_full))
    activated = low(jax.nn.silu(gate_vals) * up_vals)
    return hidden_one + low_back(matmul_t(activated, down_full))

def reference(tokens, image_starts, attn_gain, query_weight, query_bias, key_weight, key_bias, value_weight, value_bias, out_weight, mlp_gain, gate_weight, up_weight, down_weight, cotangent):
    params = tuple((array_in.astype(jnp.float32) for array_in in (attn_gain, query_weight, query_bias, key_weight, key_bias, value_weight, value_bias, out_weight, mlp_gain, gate_weight, up_weight, down_weight)))
    seq_count = image_starts.shape[0]
    width = tokens.shape[1]
    seq_tokens = tokens.astype(jnp.float32).reshape(seq_count, -1, width)

    def forward(param_set, token_set):
        seq_step = jax.checkpoint(lambda packed: one_sequence(param_set, packed[0], packed[1]))
        return lax.map(seq_step, (token_set, image_starts))
    result, pullback = jax.vjp(forward, params, seq_tokens)
    param_grads, token_grads = pullback(cotangent.astype(jnp.float32).reshape(seq_tokens.shape))
    return (result.reshape(-1, width).astype(jnp.bfloat16), token_grads.reshape(-1, width).astype(jnp.bfloat16), param_grads[0], param_grads[1], param_grads[2], param_grads[3], param_grads[4], param_grads[5], param_grads[6], param_grads[7], param_grads[8], param_grads[9], param_grads[10], param_grads[11])
```

```python
import functools

import jax
import jax.numpy as jnp
from jax import lax
from jax.experimental import pallas as pl
from jax.experimental.pallas import tpu as pltpu
from jax.sharding import Mesh, PartitionSpec as P

HD = 64
IMG = 256
KV_HEADS = 2
LANES = 128
EXTRA = 128
TILE = 256

eps = 1e-06
rope_base = 1000000.0
neg_fill = -1e30

SWAP = ((0, 1), (1, 0))
F32 = jnp.float32
BF16 = jnp.bfloat16
VMEM_CAP = 60 * 1024 * 1024


def f32(v):
    return v.astype(F32)


def bf(v):
    return v.astype(BF16)


def nn(a, b):
    return jnp.dot(a, b, preferred_element_type=F32)


def nt(a, b):
    return lax.dot_general(a, b, (((1,), (1,)), ((), ())), preferred_element_type=F32)


def tn(a, b):
    return lax.dot_general(a, b, (((0,), (0,)), ((), ())), preferred_element_type=F32)


def swap(v, axis):
    return lax.ppermute(v, axis, SWAP)


def whole():
    return pl.BlockSpec(memory_space=pltpu.VMEM)


def after(values, *earlier):
    return lax.optimization_barrier((values, earlier))[0]


def along_z(own, direct):
    count = lax.axis_size("zz")
    if not direct:
        return lax.all_gather(own, "zz", axis=0, tiled=True)
    rows = own.shape[0]
    me = lax.axis_index("zz")
    zs = jnp.zeros((count * rows, own.shape[1]), own.dtype)
    zs = lax.dynamic_update_slice(zs, own, (me * rows, 0))
    for j in range(1, count):
        got = lax.ppermute(own, "zz", [(i, i ^ j) for i in range(count)])
        zs = lax.dynamic_update_slice(zs, got, ((me ^ j) * rows, 0))
    return zs


def beside(zs):
    return swap(zs, "xx"), swap(zs, "ctx")


def diagonal(xs, ys):
    half = xs.shape[0] // 2
    return swap(ys[:half], "xx"), swap(xs[half:], "ctx")


def sum_diagonal(pieces):
    return swap(pieces[3], "xx"), swap(pieces[4], "ctx")


def two_parts(v):
    high = lax.optimization_barrier(bf(v))
    return jnp.concatenate([high, bf(v - f32(high))], axis=1)


def rounded(v, vectors):
    if not vectors:
        return bf(v)
    tail = v[:, -vectors:]
    half = vectors // 2
    return jnp.concatenate([bf(v[:, :-vectors]), two_parts(tail[:, :half] + tail[:, half:])], axis=1)


def sum_beside(pieces, got, vectors=0):
    half = pieces[3].shape[0]
    xs = jnp.concatenate([pieces[1][:half], rounded(f32(pieces[1][half:]) + f32(got[1]), vectors)], 0)
    ys = jnp.concatenate([rounded(f32(pieces[2][:half]) + f32(got[0]), vectors), pieces[2][half:]], 0)
    return swap(xs, "xx"), swap(ys, "ctx")


def sum_along_z(pieces, got, vectors=0):
    count = lax.axis_size("zz")
    me = lax.axis_index("zz")
    zs = rounded(f32(pieces[0]) + f32(got[0]) + f32(got[1]), vectors)
    if not vectors:
        return [lax.optimization_barrier(lax.psum_scatter(zs, "zz", scatter_dimension=0, tiled=True))]
    rows = zs.shape[0] // count
    parts = [lax.dynamic_slice(zs, (me * rows, 0), (rows, zs.shape[1]))]
    for j in range(1, count):
        part = lax.dynamic_slice(zs, ((me ^ j) * rows, 0), (rows, zs.shape[1]))
        parts.append(lax.ppermute(part, "zz", [(i, i ^ j) for i in range(count)]))
    return parts


def sum_pair(parts):
    own = sum(f32(p) for p in parts)
    rows = own.shape[0]
    first, second = own[: rows // 2], own[rows // 2 :]
    here = lax.axis_index("core") == 0
    return jnp.where(here, first, second), swap(jnp.where(here, second, first), "core")


def pair_rows(mine, theirs):
    got = swap(theirs, "core")
    here = lax.axis_index("core") == 0
    return jnp.where(here, jnp.concatenate([mine, got], axis=0), jnp.concatenate([got, mine], axis=0))


def tiles_of(width):
    return [(o, min(TILE, width - o)) for o in range(0, width, TILE)]


def pack_kernel(chunks, core_ref, gate_ref, up_ref, down_ref, *outs):
    core = core_ref[0]
    half = gate_ref.shape[1] // 2
    for side in range(2):
        base = jnp.where(side == 0, core, 1 - core) * half
        for (start, width), out in zip(chunks, outs[side * len(chunks) : (side + 1) * len(chunks)]):
            for o, t in tiles_of(width):
                for k, ref in enumerate((gate_ref, up_ref, down_ref)):
                    at = pl.multiple_of(base + (start + o), LANES)
                    out[:, 3 * o + k * t : 3 * o + (k + 1) * t] = ref[:, pl.ds(at, t)]


def pack(core, gate, up, down, chunks):
    rows = gate.shape[0]
    shapes = [jax.ShapeDtypeStruct((rows, 3 * w), gate.dtype) for _, w in chunks] * 2
    return pl.pallas_call(
        functools.partial(pack_kernel, chunks),
        in_specs=[pl.BlockSpec(memory_space=pltpu.SMEM)] + [whole()] * 3,
        out_specs=[whole()] * len(shapes),
        out_shape=shapes,
        name="pack",
    )(core, gate, up, down)


def unpack_kernel(chunks, core_ref, *refs):
    core = core_ref[0]
    ins, outs = refs[: 2 * len(chunks)], refs[2 * len(chunks) :]
    half = outs[0].shape[1] // 2
    for side in range(2):
        base = jnp.where(side == 0, core, 1 - core) * half
        for (start, width), ref in zip(chunks, ins[side * len(chunks) : (side + 1) * len(chunks)]):
            for o, t in tiles_of(width):
                for k, out in enumerate(outs):
                    at = pl.multiple_of(base + (start + o), LANES)
                    out[:, pl.ds(at, t)] = ref[:, 3 * o + k * t : 3 * o + (k + 1) * t]


def unpack(core, mine, theirs, chunks, width):
    rows = mine[0].shape[0]
    shapes = [jax.ShapeDtypeStruct((rows, width), F32)] * 3
    return pl.pallas_call(
        functools.partial(unpack_kernel, chunks),
        in_specs=[pl.BlockSpec(memory_space=pltpu.SMEM)] + [whole()] * (2 * len(chunks)),
        out_specs=[whole()] * 3,
        out_shape=shapes,
        name="unpack",
    )(core, *mine, *theirs)


def mlp_kernel(last_t, rows, xm, xt, cm, ct, zw, xw, yw, aw, bw, om, ot, gm, gt, dz, dx, dy, da, db,
               xs, cs, oacc, gacc, w, h, low, sem):
    step = pl.program_id(0)
    steps = pl.num_programs(0)
    tokens = xm.shape[0]
    quarter = zw.shape[0]
    half = quarter // 2

    @pl.when(step == 0)
    def _():
        copies = [
            pltpu.make_async_copy(src, dst.at[pl.ds(o, tokens)], sem.at[i])
            for i, (src, dst, o) in enumerate(((xm, xs, 0), (xt, xs, tokens), (cm, cs, 0), (ct, cs, tokens)))
        ]
        for c in copies:
            c.start()
        for c in copies:
            c.wait()

    w[0:quarter] = zw[...]
    w[quarter : 2 * quarter] = xw[...]
    w[2 * quarter : 3 * quarter] = yw[...]
    w[3 * quarter : 3 * quarter + half] = aw[...]
    w[3 * quarter + half :] = bw[...]

    def grads(t):
        for x_ref, a, b in ((xs, 0, t), (xs, t, 2 * t), (cs, 2 * t, 3 * t)):
            d = bf(tn(x_ref[...], h[:, a:b]))
            dz[:, a:b] = d[:quarter]
            dx[:, a:b] = d[quarter : 2 * quarter]
            dy[:, a:b] = d[2 * quarter : 3 * quarter]
            da[:, a:b] = d[3 * quarter : 3 * quarter + half]
            db[:, a:b] = d[3 * quarter + half :]

    def work(t):
        def block(i, carry):
            at = pl.multiple_of(i * rows, rows)
            here = pl.ds(at, rows)
            x = xs[here, :]
            g = nn(x, w[:, :t])
            u = nn(x, w[:, t : 2 * t])
            ga = nn(cs[here, :], w[:, 2 * t : 3 * t])
            sg = 0.5 * jnp.tanh(0.5 * g) + 0.5
            silu = g * sg
            h[here, 2 * t : 3 * t] = bf(silu * u)
            h[here, :t] = bf(ga * u * (sg + silu * (1.0 - sg)))
            h[here, t : 2 * t] = bf(ga * silu)
            old = step > 0
            o = nt(h[here, 2 * t : 3 * t], w[:, 2 * t : 3 * t])
            oacc[here, :] = o + jnp.where(old, oacc[here, :], 0.0)
            gn = nt(h[here, : 2 * t], w[:, : 2 * t])
            gacc[here, :] = gn + jnp.where(old, gacc[here, :], 0.0)
            return carry

        lax.fori_loop(0, 2 * tokens // rows, block, 0)

    def sums_out():
        return [
            pltpu.make_async_copy(low.at[i], dst, sem.at[i])
            for i, dst in enumerate((gt, gm, ot, om))
        ]

    def tile(t):
        work(t)

        @pl.when(step == steps - 1)
        def _():
            for i, (acc, part) in enumerate(((gacc, 1), (gacc, 0), (oacc, 1), (oacc, 0))):
                low[i] = bf(acc[pl.ds(part * tokens, tokens), :])
            for c in sums_out():
                c.start()

        grads(t)

    if last_t == TILE:
        tile(TILE)
    else:
        @pl.when(step < steps - 1)
        def _():
            tile(TILE)

        @pl.when(step == steps - 1)
        def _():
            tile(last_t)

    @pl.when(step == steps - 1)
    def _():
        for c in sums_out():
            c.wait()


def mlp(xm, xt, cm, ct, pieces, rows=1024):
    tokens, width = xm.shape
    cols = pieces[0].shape[1] // 3
    steps = pl.cdiv(cols, TILE)
    last_t = cols - (steps - 1) * TILE
    block = lambda p: pl.BlockSpec((p.shape[0], 3 * TILE), lambda i: (0, i))
    any_space = pl.BlockSpec(memory_space=pl.ANY)
    lo = jax.ShapeDtypeStruct((tokens, width), BF16)
    return pl.pallas_call(
        functools.partial(mlp_kernel, last_t, rows),
        grid=(steps,),
        in_specs=[any_space] * 4 + [block(p) for p in pieces],
        out_specs=[any_space] * 4 + [block(p) for p in pieces],
        out_shape=[lo] * 4 + [jax.ShapeDtypeStruct(p.shape, BF16) for p in pieces],
        scratch_shapes=[
            pltpu.VMEM((2 * tokens, width), BF16),
            pltpu.VMEM((2 * tokens, width), BF16),
            pltpu.VMEM((2 * tokens, width), F32),
            pltpu.VMEM((2 * tokens, width), F32),
            pltpu.VMEM((width, 3 * TILE), BF16),
            pltpu.VMEM((2 * tokens, 3 * TILE), BF16),
            pltpu.VMEM((4, tokens, width), BF16),
            pltpu.SemaphoreType.DMA((4,)),
        ],
        compiler_params=pltpu.CompilerParams(vmem_limit_bytes=VMEM_CAP),
        cost_estimate=pl.CostEstimate(flops=9 * 2 * 2 * tokens * width * cols, bytes_accessed=12 * width * cols, transcendentals=0),
        name="feed_forward",
    )(xm, xt, cm, ct, *pieces)


def spans(info_ref, qi, bq, bk, length):
    first = info_ref[0] * length + qi * bq
    last = first + bq - 1
    top = last + 1
    starts = (info_ref[1], info_ref[2])
    for s in starts:
        top = jnp.where((s <= last) & (s + IMG > first), jnp.maximum(top, s + IMG), top)
    return first, (first + 1) // bk, (top + bk - 1) // bk, starts


def allowed_tile(first, key_first, starts, bk, bq):
    kp = key_first + lax.broadcasted_iota(jnp.int32, (bk, bq), 0)
    qp = first + lax.broadcasted_iota(jnp.int32, (bk, bq), 1)
    ok = kp <= qp
    for s in starts:
        ok = ok | ((kp >= s) & (kp < s + IMG) & (qp >= s) & (qp < s + IMG))
    return ok


def stack_heads(ref, heads):
    return jnp.concatenate([ref[HD * h : HD * (h + 1), :] for h in range(heads)], axis=1)


def attn_fwd_kernel(bk, info_ref, q_ref, loc_ref, rem_ref, o_ref, rest_ref, lse_ref, k3, vt3):
    qi = pl.program_id(0)
    length = loc_ref.shape[1]
    blocks = length // bk
    heads = q_ref.shape[0] // HD
    bq = q_ref.shape[1]

    @pl.when(qi == 0)
    def _():
        for side, ref in enumerate((loc_ref, rem_ref)):
            for b in range(blocks):
                cols = slice(b * bk, (b + 1) * bk)
                k3[side * blocks + b] = jnp.transpose(ref[:HD, cols])
                vt3[side * blocks + b, :HD] = ref[HD:, cols]
                vt3[side * blocks + b, HD:] = jnp.ones((16, bk), BF16)

    first, n_full, n_all, starts = spans(info_ref, qi, bq, bk, length)
    q = stack_heads(q_ref, heads)
    width = heads * bq
    shift = info_ref[0] * blocks

    def step(b, carry, masked):
        top, acc = carry
        slot = lax.rem(b + shift, 2 * blocks)
        s = nn(k3[slot], q)
        if masked:
            ok = allowed_tile(first, b * bk, starts, bk, bq)
            s = jnp.concatenate([jnp.where(ok, s[:, h * bq : (h + 1) * bq], neg_fill) for h in range(heads)], axis=1)
        new_top = jnp.maximum(top, jnp.max(s, axis=0, keepdims=True))
        p = jnp.exp(s - new_top)
        scale = jnp.exp(top - new_top)
        acc = acc * scale + nn(vt3[slot], bf(p))
        return new_top, acc

    carry = (jnp.full((1, width), neg_fill, F32), jnp.zeros((HD + 16, width), F32))
    carry = lax.fori_loop(0, n_full, functools.partial(step, masked=False), carry)
    top, acc = lax.fori_loop(n_full, n_all, functools.partial(step, masked=True), carry)
    total = acc[HD : HD + 1]
    out = acc[:HD] / total
    low = bf(out)
    rest = bf(out - f32(low))
    for h in range(heads):
        o_ref[HD * h : HD * (h + 1), :] = low[:, h * bq : (h + 1) * bq]
        rest_ref[HD * h : HD * (h + 1), :] = rest[:, h * bq : (h + 1) * bq]
    lse_ref[...] = (top + jnp.log(total)).reshape(lse_ref.shape)


def attn_fwd(info, q, loc, rem, bq, bk):
    group, length = q.shape
    blocks = length // bq
    width = group // HD * bq
    return pl.pallas_call(
        functools.partial(attn_fwd_kernel, bk),
        grid=(blocks,),
        in_specs=[
            pl.BlockSpec(memory_space=pltpu.SMEM),
            pl.BlockSpec((group, bq), lambda i: (0, i)),
            whole(),
            whole(),
        ],
        out_specs=[
            pl.BlockSpec((group, bq), lambda i: (0, i)),
            pl.BlockSpec((group, bq), lambda i: (0, i)),
            pl.BlockSpec((1, 1, width), lambda i: (i, 0, 0)),
        ],
        out_shape=[
            jax.ShapeDtypeStruct((group, length), BF16),
            jax.ShapeDtypeStruct((group, length), BF16),
            jax.ShapeDtypeStruct((blocks, 1, width), F32),
        ],
        scratch_shapes=[
            pltpu.VMEM((2 * length // bk, bk, HD), BF16),
            pltpu.VMEM((2 * length // bk, HD + 16, bk), BF16),
        ],
        compiler_params=pltpu.CompilerParams(vmem_limit_bytes=VMEM_CAP),
        cost_estimate=pl.CostEstimate(flops=16 * group * length * length, bytes_accessed=8 * group * length, transcendentals=group * length * length // HD),
        name="attention",
    )(info, q, loc, rem)


def attn_bwd_kernel(bk, info_ref, q_ref, do_ref, o_ref, rest_ref, lse_ref, loc_ref, rem_ref, rope_q, rope_l, rope_r,
                    dq_ref, dloc_ref, drem_ref, sum_ref, k3, kt3, v3, dk3, dv3):
    qi = pl.program_id(0)
    length = loc_ref.shape[1]
    blocks = length // bk
    heads = q_ref.shape[0] // HD
    bq = q_ref.shape[1]
    hd = HD // 2

    @pl.when(qi == 0)
    def _():
        for side, ref in enumerate((loc_ref, rem_ref)):
            for b in range(blocks):
                cols = slice(b * bk, (b + 1) * bk)
                k3[side * blocks + b] = jnp.transpose(ref[:HD, cols])
                kt3[side * blocks + b] = ref[:HD, cols]
                v3[side * blocks + b] = jnp.transpose(ref[HD:, cols])
        dk3[...] = jnp.zeros_like(dk3)
        dv3[...] = jnp.zeros_like(dv3)

    first, n_full, n_all, starts = spans(info_ref, qi, bq, bk, length)
    q = stack_heads(q_ref, heads)
    do = stack_heads(do_ref, heads)
    o = f32(stack_heads(o_ref, heads)) + f32(stack_heads(rest_ref, heads))
    delta = jnp.sum(f32(do) * o, axis=0, keepdims=True)
    lse = lse_ref[...].reshape(1, heads * bq)
    shift = info_ref[0] * blocks

    def step(b, dq, masked):
        slot = lax.rem(b + shift, 2 * blocks)
        s = nn(k3[slot], q)
        if masked:
            ok = allowed_tile(first, b * bk, starts, bk, bq)
            s = jnp.concatenate([jnp.where(ok, s[:, h * bq : (h + 1) * bq], neg_fill) for h in range(heads)], axis=1)
        p = jnp.exp(s - lse)
        dp = nn(v3[slot], do)
        ds = bf(p * (dp - delta))
        dv3[slot] += nt(do, bf(p))
        dk3[slot] += nt(q, ds)
        return dq + nn(kt3[slot], ds)

    dq = jnp.zeros((HD, heads * bq), F32)
    dq = lax.fori_loop(0, n_full, functools.partial(step, masked=False), dq)
    dq = lax.fori_loop(n_full, n_all, functools.partial(step, masked=True), dq)

    def back(v, table):
        cos, sin = table[:hd], table[hd:]
        a, b = v[:hd], v[hd:]
        return jnp.concatenate([a * cos + b * sin, b * cos - a * sin], axis=0)

    scale = HD**-0.5
    table = rope_q[...]
    for h in range(heads):
        dq_ref[HD * h : HD * (h + 1), :] = bf(back(dq[:, h * bq : (h + 1) * bq] * scale, table))

    @pl.when(qi == pl.num_programs(0) - 1)
    def _():
        fold = jnp.zeros(sum_ref.shape, F32)
        for side, (ref, rope) in enumerate(((dloc_ref, rope_l), (drem_ref, rope_r))):
            for b in range(blocks):
                cols = slice(b * bk, (b + 1) * bk)
                both = jnp.concatenate([back(dk3[side * blocks + b], rope[:, cols]), dv3[side * blocks + b]], axis=0)
                ref[:, cols] = both.astype(ref.dtype)
                for o in range(0, bk, LANES):
                    fold = fold + both[:, o : o + LANES]
        sum_ref[...] = fold


def attn_bwd(info, q, do, o, rest, lse, loc, rem, rope_loc, rope_rem, bq, bk):
    group, length = q.shape
    blocks = length // bq
    width = group // HD * bq
    rows = pl.BlockSpec((group, bq), lambda i: (0, i))
    return pl.pallas_call(
        functools.partial(attn_bwd_kernel, bk),
        grid=(blocks,),
        in_specs=[
            pl.BlockSpec(memory_space=pltpu.SMEM),
            rows, rows, rows, rows,
            pl.BlockSpec((1, 1, width), lambda i: (i, 0, 0)),
            whole(), whole(),
            pl.BlockSpec((HD, bq), lambda i: (0, i)),
            whole(), whole(),
        ],
        out_specs=[rows, whole(), whole(), whole()],
        out_shape=[
            jax.ShapeDtypeStruct((group, length), BF16),
            jax.ShapeDtypeStruct(loc.shape, F32),
            jax.ShapeDtypeStruct(loc.shape, BF16),
            jax.ShapeDtypeStruct((loc.shape[0], LANES), F32),
        ],
        scratch_shapes=[
            pltpu.VMEM((2 * length // bk, bk, HD), BF16),
            pltpu.VMEM((2 * length // bk, HD, bk), BF16),
            pltpu.VMEM((2 * length // bk, bk, HD), BF16),
            pltpu.VMEM((2 * length // bk, HD, bk), F32),
            pltpu.VMEM((2 * length // bk, HD, bk), F32),
        ],
        compiler_params=pltpu.CompilerParams(vmem_limit_bytes=VMEM_CAP),
        cost_estimate=pl.CostEstimate(flops=40 * group * length * length, bytes_accessed=16 * group * length, transcendentals=group * length * length // HD),
        name="attention_back",
    )(info, q, do, o, rest, lse, loc, rem, rope_loc, rope_loc, rope_rem)


def rope_table(first, length):
    half = HD // 2
    inverse = rope_base ** (-(jnp.arange(half).astype(F32) * 2.0 / HD))
    angles = inverse[:, None] * f32(first + jnp.arange(length, dtype=jnp.int32))[None, :]
    return jnp.concatenate([jnp.cos(angles), jnp.sin(angles)], axis=0)


def rope(v, table):
    half = HD // 2
    shaped = v.reshape(-1, 2, half, v.shape[1])
    cos, sin = table[None, :half], table[None, half:]
    a, b = shaped[:, 0], shaped[:, 1]
    return jnp.stack([a * cos - b * sin, b * cos + a * sin], axis=1).reshape(v.shape)


def device_order(rows, count):
    p = jnp.arange(8 * count * rows, dtype=jnp.int32)
    q = p // (count * 2 * rows)
    z = (p // (2 * rows)) % count
    c = (p // rows) % 2
    x_rel = ((q == 1) | (q == 3)).astype(jnp.int32)
    y_rel = (q >= 2).astype(jnp.int32)
    chip = z * 2 + (lax.axis_index("xx") ^ x_rel)
    flat = (chip * 2 + c) * 2 + (lax.axis_index("ctx") ^ y_rel)
    return flat * rows + p % rows


def column(v, rows):
    return jnp.pad(v, (0, rows - v.shape[0]))[:, None]


def shards(
    tokens, image_starts, attn_gain, query_weight, query_bias, key_weight, key_bias, value_weight, value_bias,
    out_weight, mlp_gain, gate_weight, up_weight, down_weight, cotangent,
):
    length, width = tokens.shape
    count = lax.axis_size("zz")
    devices = 8 * count
    rows = width // devices
    core = lax.axis_index("core")
    ctx = lax.axis_index("ctx")
    core_arr = core.reshape(1).astype(jnp.int32)
    feat = query_weight.shape[1]
    kv_feat = key_weight.shape[1]
    ff = gate_weight.shape[1]
    half_ff = ff // 2
    units = half_ff // LANES
    cuts = [0, units // 5 * 2 + 2, units]
    chunks = tuple((a * LANES, (b - a) * LANES) for a, b in zip(cuts, cuts[1:]))
    n = len(chunks)
    own_first = core == 0

    extras = jnp.concatenate(
        [column(v, rows) for v in (attn_gain, mlp_gain, query_bias, key_bias, value_bias)]
        + [jnp.zeros((rows, EXTRA - 5), BF16)], axis=1)
    fh, kh = feat // 2, kv_feat // 2
    sides = [
        jnp.concatenate([query_weight[:, s * fh : (s + 1) * fh], key_weight[:, s * kh : (s + 1) * kh],
                         value_weight[:, s * kh : (s + 1) * kh], out_weight[:, s * fh : (s + 1) * fh], extras], axis=1)
        for s in range(2)
    ]
    a_own = pair_rows(jnp.where(own_first, sides[0], sides[1]), jnp.where(own_first, sides[1], sides[0]))
    tokens, cotangent = after((tokens, cotangent), a_own)
    a_zs = along_z(a_own, True)
    gate_weight, up_weight, down_weight = after((gate_weight, up_weight, down_weight), a_own)
    packed = pack(core_arr, gate_weight, up_weight, down_weight, chunks)
    own = [pair_rows(packed[i], packed[n + i]) for i in range(n)]
    f_zs = [along_z(v, False) for v in own]

    natural = device_order(rows, count)
    to_dev = bf(jnp.arange(width, dtype=jnp.int32)[:, None] == natural[None, :])
    x = nn(tokens, to_dev)
    r1 = lax.rsqrt(jnp.mean(x * x, axis=-1, keepdims=True) + eps)
    table = rope_table(ctx * length, length)
    table_rem = rope_table((1 - ctx) * length, length)

    a_xs, a_ys = beside(a_zs)
    a_pieces = [a_zs, a_xs, a_ys, *diagonal(a_xs, a_ys)]
    w_mine = jnp.concatenate(a_pieces, axis=0)
    w_side = [w_mine, swap(w_mine, "core")]

    q0, k0, v0, o0, e0 = 0, fh, fh + kh, fh + 2 * kh, 2 * fh + 2 * kh
    extra_rel = w_mine[:, e0:]
    gains = jnp.transpose(f32(extra_rel[:, :2]))
    gain_attn, gain_mlp = gains[0:1], gains[1:2]
    bias_nat = nn(to_dev, extra_rel)
    q_bias = bias_nat[:, 2]
    kv_rows = kv_feat // devices
    k_bias = bias_nat[:, 3].reshape(devices, rows)[:, :kv_rows].reshape(-1)
    v_bias = bias_nat[:, 4].reshape(devices, rows)[:, :kv_rows].reshape(-1)

    def by_side(v):
        lo, hi = v[: v.shape[0] // 2], v[v.shape[0] // 2 :]
        return jnp.where(own_first, lo, hi), jnp.where(own_first, hi, lo)

    normed_one = bf(x * r1 * gain_attn)
    keys_values = []
    for w_all, kb, vb in zip(w_side, by_side(k_bias), by_side(v_bias)):
        kv = lax.dot_general(w_all[:, k0:o0], normed_one, (((0,), (1,)), ((), ())), preferred_element_type=F32)
        kv = kv + jnp.concatenate([kb, vb])[:, None]
        keys_values.append(jnp.concatenate([bf(rope(kv[:kh], table)), bf(kv[kh:])], axis=0))
    kv_rem = swap(jnp.concatenate(keys_values, axis=0), "ctx")
    kv_rem = [kv_rem[: 2 * kh], kv_rem[2 * kh :]]
    queries = []
    for w_all, qb in zip(w_side, by_side(q_bias)):
        q = lax.dot_general(w_all[:, :k0], after(normed_one, *keys_values), (((0,), (1,)), ((), ())), preferred_element_type=F32)
        queries.append(bf(rope(q + qb[:, None], table) * HD**-0.5))
    f_xy = [None] * n
    f_diag = [None] * n
    f_xs = swap(after(f_zs[0], normed_one), "xx")
    f_ys = swap(after(f_zs[0], *kv_rem), "ctx")
    f_xy[0] = (f_xs, f_ys)

    info = jnp.concatenate([ctx.reshape(1).astype(jnp.int32), image_starts[0]])
    bq = min(256, length)
    bk = min(256, length)
    queries[0] = after(queries[0], f_zs[0])
    att0, rest0, lse0 = attn_fwd(info, queries[0], keys_values[0], kv_rem[0], bq, bk)
    f_xy[0] = after(f_xy[0], att0)
    f_diag[0] = diagonal(*f_xy[0])
    f_zs[1] = after(f_zs[1], att0)
    f_xy[1] = beside(f_zs[1])
    queries[1] = after(queries[1], f_xy[0], f_zs[1])
    att1, rest1, lse1 = attn_fwd(info, queries[1], keys_values[1], kv_rem[1], bq, bk)
    f_xy[1] = after(f_xy[1], att1)
    f_diag[1] = diagonal(*f_xy[1])
    for i in range(2, n):
        f_zs[i] = after(f_zs[i], att1)
        f_xy[i] = beside(f_zs[i])
    attended, rest, lse = [att0, att1], [rest0, rest1], [lse0, lse1]

    cotangent = after(cotangent, att0)
    cot = bf(nn(cotangent, to_dev))
    cot_theirs = swap(cot, "core")
    hidden = x
    for a, w_all in zip(attended, w_side):
        hidden = hidden + lax.dot_general(a, w_all[:, o0:e0], (((0,), (1,)), ((), ())), preferred_element_type=F32)
    r2 = lax.rsqrt(jnp.mean(hidden * hidden, axis=-1, keepdims=True) + eps)
    normed_two = bf(hidden * r2 * gain_mlp)
    normed_theirs = swap(normed_two, "core")

    results, got_d, got_b, got_z = [], [None] * n, [None] * n, [None] * n
    x_in = normed_two
    for i in range(n):
        r = mlp(x_in, normed_theirs, cot, cot_theirs, [f_zs[i], *f_xy[i], *f_diag[i]])
        results.append(r)
        x_in = after(normed_two, r[2])
        if i + 2 < n:
            f_xy[i + 2] = after(f_xy[i + 2], r[2])
            f_diag[i + 2] = diagonal(*f_xy[i + 2])
        got_d[i] = sum_diagonal(r[4:])
        if i > 0:
            got_d[i - 1] = after(got_d[i - 1], r[2])
            got_b[i - 1] = sum_beside(results[i - 1][4:], got_d[i - 1])

    def total(a, b):
        mine = sum(f32(r[a]) for r in results)
        return mine + f32(swap(bf(sum(f32(r[b]) for r in results)), "core"))

    grad_two = total(2, 3)
    mlp_gain_grad = jnp.sum(grad_two * hidden * r2, axis=0)
    u = grad_two * gain_mlp
    grad_hidden = f32(cot) + r2 * u - hidden * (r2 * r2 * r2) * jnp.mean(u * hidden, axis=-1, keepdims=True)
    grad_attn = bf(grad_hidden)
    grad_mixed = [
        bf(lax.dot_general(w_all[:, o0:e0], grad_attn, (((0,), (1,)), ((), ())), preferred_element_type=F32)) for w_all in w_side
    ]

    lows, d_sums = [], []
    back = [None, None]
    for s in range(2):
        do = grad_mixed[s]
        if s == 1:
            do = after(do, back[0][0])
            for i in range(n - 1):
                got_b[i] = after(got_b[i], back[0][0])
                got_z[i] = sum_along_z(results[i][4:], got_b[i])
            got_d[n - 1] = after(got_d[n - 1], back[0][0])
            got_b[n - 1] = sum_beside(results[n - 1][4:], got_d[n - 1])
        back[s] = attn_bwd(info, queries[s], do, attended[s], rest[s], lse[s], keys_values[s], kv_rem[s], table, table_rem, bq, bk)
    got_b[n - 1] = after(got_b[n - 1], back[1][0])
    got_z[n - 1] = sum_along_z(results[n - 1][4:], got_b[n - 1])
    for s in range(2):
        query_low, d_loc, d_rem, _ = back[s]
        kv_low = bf(d_loc + f32(swap(d_rem, "ctx")))
        lows.append(jnp.concatenate([query_low, kv_low], axis=0))

    out_sum = total(0, 1)
    output = bf(nt(bf(hidden + out_sum), to_dev))
    mlp_out = [sum_pair(z) for z in got_z]
    gate_grad, up_grad, down_grad = unpack(core_arr, [m[0] for m in mlp_out], [m[1] for m in mlp_out], chunks, ff)

    out_grad = [lax.dot_general(grad_attn, a, (((0,), (1,)), ((), ())), preferred_element_type=F32) for a in attended]
    grad_one = 0.0
    for low, w_all in zip(lows, w_side):
        grad_one = grad_one + lax.dot_general(low, w_all[:, :o0], (((0,), (1,)), ((), ())), preferred_element_type=F32)
    w = grad_one * gain_attn
    tokens_grad_dev = grad_hidden + r1 * w - x * (r1 * r1 * r1) * jnp.mean(w * x, axis=-1, keepdims=True)
    tokens_grad = bf(nt(bf(tokens_grad_dev), to_dev))
    attn_gain_grad = jnp.sum(grad_one * x * r1, axis=0)
    qkv_grad = [lax.dot_general(normed_one, low, (((0,), (1,)), ((), ())), preferred_element_type=F32) for low in lows]
    bias_grad = [jnp.concatenate([jnp.sum(f32(b[0]), axis=1), jnp.sum(b[3], axis=1)]) for b in back]

    def whole_order(a, b):
        return jnp.where(own_first, jnp.concatenate([a, b]), jnp.concatenate([b, a]))

    def spread(v):
        return jnp.pad(v.reshape(devices, -1), ((0, 0), (0, rows - v.shape[0] // devices))).reshape(-1)

    qb, kb, vb = [whole_order(bias_grad[0][a:b], bias_grad[1][a:b]) for a, b in ((q0, k0), (k0, v0), (v0, o0))]
    nat_cols = jnp.stack([qb, spread(kb), spread(vb)], axis=0)
    dev_cols = nn(two_parts(nat_cols.T).T, to_dev)
    dev_cols = dev_cols[:3] + dev_cols[3:]
    vec_cols = jnp.concatenate([attn_gain_grad[None], mlp_gain_grad[None], dev_cols, jnp.zeros((EXTRA // 2 - 5, width), F32)], axis=0)
    extra_grad = two_parts(jnp.transpose(vec_cols))
    g_mine = jnp.concatenate([bf(qkv_grad[0]), bf(out_grad[0]), extra_grad], axis=1)
    g_theirs = jnp.concatenate([bf(qkv_grad[1]), bf(out_grad[1])], axis=1)
    got = swap(g_theirs, "core")
    g_sum = jnp.concatenate([bf(f32(g_mine[:, :e0]) + f32(got)), g_mine[:, e0:]], axis=1)
    quarter = width // 4
    bounds = [0, quarter, 2 * quarter, 3 * quarter, 3 * quarter + quarter // 2, width]
    g_pieces = [g_sum[a:b] for a, b in zip(bounds, bounds[1:])]
    g_got = sum_beside(g_pieces, sum_diagonal(g_pieces), EXTRA)
    a_mine, a_theirs = sum_pair(sum_along_z(g_pieces, g_got, EXTRA))

    def natural_cols(a, b):
        lo, hi = a_mine[:, a:b], a_theirs[:, a:b]
        return jnp.where(own_first, jnp.concatenate([lo, hi], axis=1), jnp.concatenate([hi, lo], axis=1))

    extra = a_mine[:, e0:] + a_theirs[:, e0:]
    extra = extra[:, : EXTRA // 2] + extra[:, EXTRA // 2 :]
    return (
        output,
        tokens_grad,
        extra[:, 0],
        natural_cols(q0, k0),
        extra[:, 2],
        natural_cols(k0, v0),
        extra[:kv_rows, 3],
        natural_cols(v0, o0),
        extra[:kv_rows, 4],
        natural_cols(o0, e0),
        extra[:, 1],
        gate_grad,
        up_grad,
        down_grad,
    )


def solution(mesh):
    dp, ctx = mesh.devices.shape
    fine = Mesh(mesh.devices.reshape(dp // 4, 2, 2, ctx), ("zz", "xx", "core", "ctx"))
    every = ("zz", "xx", "core", "ctx")
    mat, vec = P(every, None), P(every)
    placed = (mat, P(("zz", "xx", "core"), None), vec, mat, vec, mat, vec, mat, vec, mat, vec, mat, mat, mat, mat)
    outs = (mat, mat, vec, mat, vec, mat, vec, mat, vec, mat, vec, mat, mat, mat)
    return jax.shard_map(shards, mesh=fine, in_specs=placed, out_specs=outs, check_vma=False)
```

```python
import functools

import jax
import jax.numpy as jnp
from jax import lax
from jax.experimental import pallas as pl
from jax.experimental.pallas import tpu as pltpu
from jax.sharding import Mesh, PartitionSpec as P

HD = 64
IMG = 256
KV_HEADS = 2
LANES = 128
EXTRA = 128
TILE = 256

eps = 1e-06
rope_base = 1000000.0
neg_fill = -1e30

SWAP = ((0, 1), (1, 0))
F32 = jnp.float32
BF16 = jnp.bfloat16
VMEM_CAP = 60 * 1024 * 1024


def f32(v):
    return v.astype(F32)


def bf(v):
    return v.astype(BF16)


def nn(a, b):
    return jnp.dot(a, b, preferred_element_type=F32)


def nt(a, b):
    return lax.dot_general(a, b, (((1,), (1,)), ((), ())), preferred_element_type=F32)


def tn(a, b):
    return lax.dot_general(a, b, (((0,), (0,)), ((), ())), preferred_element_type=F32)


def swap(v, axis):
    return lax.ppermute(v, axis, SWAP)


def whole():
    return pl.BlockSpec(memory_space=pltpu.VMEM)


def after(values, *earlier):
    return lax.optimization_barrier((values, earlier))[0]


def along_z(own, direct):
    count = lax.axis_size("zz")
    if not direct:
        return lax.all_gather(own, "zz", axis=0, tiled=True)
    rows = own.shape[0]
    me = lax.axis_index("zz")
    zs = jnp.zeros((count * rows, own.shape[1]), own.dtype)
    zs = lax.dynamic_update_slice(zs, own, (me * rows, 0))
    for j in range(1, count):
        got = lax.ppermute(own, "zz", [(i, i ^ j) for i in range(count)])
        zs = lax.dynamic_update_slice(zs, got, ((me ^ j) * rows, 0))
    return zs


def beside(zs):
    return swap(zs, "xx"), swap(zs, "ctx")


def diagonal(xs, ys):
    half = xs.shape[0] // 2
    return swap(ys[:half], "xx"), swap(xs[half:], "ctx")


def sum_diagonal(pieces):
    return swap(pieces[3], "xx"), swap(pieces[4], "ctx")


def two_parts(v):
    high = lax.optimization_barrier(bf(v))
    return jnp.concatenate([high, bf(v - f32(high))], axis=1)


def rounded(v, vectors):
    if not vectors:
        return bf(v)
    tail = v[:, -vectors:]
    half = vectors // 2
    return jnp.concatenate([bf(v[:, :-vectors]), two_parts(tail[:, :half] + tail[:, half:])], axis=1)


def sum_beside(pieces, got, vectors=0):
    half = pieces[3].shape[0]
    xs = rounded(f32(pieces[1]) + jnp.pad(f32(got[1]), ((half, 0), (0, 0))), vectors)
    ys = rounded(f32(pieces[2]) + jnp.pad(f32(got[0]), ((0, half), (0, 0))), vectors)
    return swap(xs, "xx"), swap(ys, "ctx")


def sum_own(pieces, got, vectors=0):
    return rounded(f32(pieces[0]) + f32(got[0]) + f32(got[1]), vectors)


def sum_along_z(zs, direct):
    count = lax.axis_size("zz")
    me = lax.axis_index("zz")
    if not direct:
        return [lax.optimization_barrier(lax.psum_scatter(zs, "zz", scatter_dimension=0, tiled=True))]
    rows = zs.shape[0] // count
    parts = [lax.dynamic_slice(zs, (me * rows, 0), (rows, zs.shape[1]))]
    for j in range(1, count):
        part = lax.dynamic_slice(zs, ((me ^ j) * rows, 0), (rows, zs.shape[1]))
        parts.append(lax.ppermute(part, "zz", [(i, i ^ j) for i in range(count)]))
    return parts


def sum_pair(parts):
    own = sum(f32(p) for p in parts)
    rows = own.shape[0]
    first, second = own[: rows // 2], own[rows // 2 :]
    here = lax.axis_index("core") == 0
    return jnp.where(here, first, second), swap(jnp.where(here, second, first), "core")


def pair_rows(mine, theirs):
    got = swap(theirs, "core")
    here = lax.axis_index("core") == 0
    return jnp.where(here, jnp.concatenate([mine, got], axis=0), jnp.concatenate([got, mine], axis=0))


def tiles_of(width):
    return [(o, min(TILE, width - o)) for o in range(0, width, TILE)]


def pack_kernel(chunks, core_ref, gate_ref, up_ref, down_ref, *outs):
    core = core_ref[0]
    half = gate_ref.shape[1] // 2
    for side in range(2):
        base = jnp.where(side == 0, core, 1 - core) * half
        for (start, width), out in zip(chunks, outs[side * len(chunks) : (side + 1) * len(chunks)]):
            for o, t in tiles_of(width):
                for k, ref in enumerate((gate_ref, up_ref, down_ref)):
                    at = pl.multiple_of(base + (start + o), LANES)
                    out[:, 3 * o + k * t : 3 * o + (k + 1) * t] = ref[:, pl.ds(at, t)]


def pack(core, gate, up, down, chunks):
    rows = gate.shape[0]
    shapes = [jax.ShapeDtypeStruct((rows, 3 * w), gate.dtype) for _, w in chunks] * 2
    return pl.pallas_call(
        functools.partial(pack_kernel, chunks),
        in_specs=[pl.BlockSpec(memory_space=pltpu.SMEM)] + [whole()] * 3,
        out_specs=[whole()] * len(shapes),
        out_shape=shapes,
        name="pack",
    )(core, gate, up, down)


def unpack_kernel(chunks, core_ref, *refs):
    core = core_ref[0]
    ins, outs = refs[: 2 * len(chunks)], refs[2 * len(chunks) :]
    half = outs[0].shape[1] // 2
    for side in range(2):
        base = jnp.where(side == 0, core, 1 - core) * half
        for (start, width), ref in zip(chunks, ins[side * len(chunks) : (side + 1) * len(chunks)]):
            for o, t in tiles_of(width):
                for k, out in enumerate(outs):
                    at = pl.multiple_of(base + (start + o), LANES)
                    out[:, pl.ds(at, t)] = ref[:, 3 * o + k * t : 3 * o + (k + 1) * t]


def unpack(core, mine, theirs, chunks, width):
    rows = mine[0].shape[0]
    shapes = [jax.ShapeDtypeStruct((rows, width), F32)] * 3
    return pl.pallas_call(
        functools.partial(unpack_kernel, chunks),
        in_specs=[pl.BlockSpec(memory_space=pltpu.SMEM)] + [whole()] * (2 * len(chunks)),
        out_specs=[whole()] * 3,
        out_shape=shapes,
        name="unpack",
    )(core, *mine, *theirs)


def mlp_kernel(last_t, rows, xm, xt, cm, ct, zw, xw, yw, aw, bw, om, ot, gm, gt, dz, dx, dy, da, db,
               xs, cs, oacc, gacc, w, h, low, sem):
    step = pl.program_id(0)
    steps = pl.num_programs(0)
    tokens = xm.shape[0]
    quarter = zw.shape[0]
    half = quarter // 2

    @pl.when(step == 0)
    def _():
        copies = [
            pltpu.make_async_copy(src, dst.at[pl.ds(o, tokens)], sem.at[i])
            for i, (src, dst, o) in enumerate(((xm, xs, 0), (xt, xs, tokens), (cm, cs, 0), (ct, cs, tokens)))
        ]
        for c in copies:
            c.start()
        for c in copies:
            c.wait()

    w[0:quarter] = zw[...]
    w[quarter : 2 * quarter] = xw[...]
    w[2 * quarter : 3 * quarter] = yw[...]
    w[3 * quarter : 3 * quarter + half] = aw[...]
    w[3 * quarter + half :] = bw[...]

    def grads(t):
        for x_ref, a, b in ((xs, 0, t), (xs, t, 2 * t), (cs, 2 * t, 3 * t)):
            d = bf(tn(x_ref[...], h[:, a:b]))
            dz[:, a:b] = d[:quarter]
            dx[:, a:b] = d[quarter : 2 * quarter]
            dy[:, a:b] = d[2 * quarter : 3 * quarter]
            da[:, a:b] = d[3 * quarter : 3 * quarter + half]
            db[:, a:b] = d[3 * quarter + half :]

    def work(t):
        def block(i, carry):
            at = pl.multiple_of(i * rows, rows)
            here = pl.ds(at, rows)
            x = xs[here, :]
            g = nn(x, w[:, :t])
            u = nn(x, w[:, t : 2 * t])
            ga = nn(cs[here, :], w[:, 2 * t : 3 * t])
            sg = 0.5 * jnp.tanh(0.5 * g) + 0.5
            silu = g * sg
            h[here, 2 * t : 3 * t] = bf(silu * u)
            h[here, :t] = bf(ga * u * (sg + silu * (1.0 - sg)))
            h[here, t : 2 * t] = bf(ga * silu)
            old = step > 0
            o = nt(h[here, 2 * t : 3 * t], w[:, 2 * t : 3 * t])
            oacc[here, :] = o + jnp.where(old, oacc[here, :], 0.0)
            gn = nt(h[here, : 2 * t], w[:, : 2 * t])
            gacc[here, :] = gn + jnp.where(old, gacc[here, :], 0.0)
            return carry

        lax.fori_loop(0, 2 * tokens // rows, block, 0)

    def sums_out():
        return [
            pltpu.make_async_copy(low.at[i], dst, sem.at[i])
            for i, dst in enumerate((gt, gm, ot, om))
        ]

    def tile(t):
        work(t)

        @pl.when(step == steps - 1)
        def _():
            for i, (acc, part) in enumerate(((gacc, 1), (gacc, 0), (oacc, 1), (oacc, 0))):
                low[i] = bf(acc[pl.ds(part * tokens, tokens), :])
            for c in sums_out():
                c.start()

        grads(t)

    if last_t == TILE:
        tile(TILE)
    else:
        @pl.when(step < steps - 1)
        def _():
            tile(TILE)

        @pl.when(step == steps - 1)
        def _():
            tile(last_t)

    @pl.when(step == steps - 1)
    def _():
        for c in sums_out():
            c.wait()


def mlp(xm, xt, cm, ct, pieces, rows=1024):
    tokens, width = xm.shape
    cols = pieces[0].shape[1] // 3
    steps = pl.cdiv(cols, TILE)
    last_t = cols - (steps - 1) * TILE
    block = lambda p: pl.BlockSpec((p.shape[0], 3 * TILE), lambda i: (0, i))
    any_space = pl.BlockSpec(memory_space=pl.ANY)
    lo = jax.ShapeDtypeStruct((tokens, width), BF16)
    return pl.pallas_call(
        functools.partial(mlp_kernel, last_t, rows),
        grid=(steps,),
        in_specs=[any_space] * 4 + [block(p) for p in pieces],
        out_specs=[any_space] * 4 + [block(p) for p in pieces],
        out_shape=[lo] * 4 + [jax.ShapeDtypeStruct(p.shape, BF16) for p in pieces],
        scratch_shapes=[
            pltpu.VMEM((2 * tokens, width), BF16),
            pltpu.VMEM((2 * tokens, width), BF16),
            pltpu.VMEM((2 * tokens, width), F32),
            pltpu.VMEM((2 * tokens, width), F32),
            pltpu.VMEM((width, 3 * TILE), BF16),
            pltpu.VMEM((2 * tokens, 3 * TILE), BF16),
            pltpu.VMEM((4, tokens, width), BF16),
            pltpu.SemaphoreType.DMA((4,)),
        ],
        compiler_params=pltpu.CompilerParams(vmem_limit_bytes=VMEM_CAP),
        cost_estimate=pl.CostEstimate(flops=9 * 2 * 2 * tokens * width * cols, bytes_accessed=12 * width * cols, transcendentals=0),
        name="feed_forward",
    )(xm, xt, cm, ct, *pieces)


def spans(info_ref, qi, bq, bk, length):
    first = info_ref[0] * length + qi * bq
    last = first + bq - 1
    top = last + 1
    starts = (info_ref[1], info_ref[2])
    for s in starts:
        top = jnp.where((s <= last) & (s + IMG > first), jnp.maximum(top, s + IMG), top)
    return first, (first + 1) // bk, (top + bk - 1) // bk, starts


def allowed_tile(first, key_first, starts, bk, bq):
    kp = key_first + lax.broadcasted_iota(jnp.int32, (bk, bq), 0)
    qp = first + lax.broadcasted_iota(jnp.int32, (bk, bq), 1)
    ok = kp <= qp
    for s in starts:
        ok = ok | ((kp >= s) & (kp < s + IMG) & (qp >= s) & (qp < s + IMG))
    return ok


def stack_heads(ref, heads):
    return jnp.concatenate([ref[HD * h : HD * (h + 1), :] for h in range(heads)], axis=1)


def attn_fwd_kernel(bk, info_ref, q_ref, loc_ref, rem_ref, o_ref, rest_ref, lse_ref, k3, vt3):
    qi = pl.program_id(0)
    length = loc_ref.shape[1]
    blocks = length // bk
    heads = q_ref.shape[0] // HD
    bq = q_ref.shape[1]

    @pl.when(qi == 0)
    def _():
        for side, ref in enumerate((loc_ref, rem_ref)):
            for b in range(blocks):
                cols = slice(b * bk, (b + 1) * bk)
                k3[side * blocks + b] = jnp.transpose(ref[:HD, cols])
                vt3[side * blocks + b, :HD] = ref[HD:, cols]
                vt3[side * blocks + b, HD:] = jnp.ones((16, bk), BF16)

    first, n_full, n_all, starts = spans(info_ref, qi, bq, bk, length)
    q = stack_heads(q_ref, heads)
    width = heads * bq
    shift = info_ref[0] * blocks

    def step(b, carry, masked):
        top, acc = carry
        slot = lax.rem(b + shift, 2 * blocks)
        s = nn(k3[slot], q)
        if masked:
            ok = allowed_tile(first, b * bk, starts, bk, bq)
            s = jnp.concatenate([jnp.where(ok, s[:, h * bq : (h + 1) * bq], neg_fill) for h in range(heads)], axis=1)
        new_top = jnp.maximum(top, jnp.max(s, axis=0, keepdims=True))
        p = jnp.exp(s - new_top)
        scale = jnp.exp(top - new_top)
        acc = acc * scale + nn(vt3[slot], bf(p))
        return new_top, acc

    carry = (jnp.full((1, width), neg_fill, F32), jnp.zeros((HD + 16, width), F32))
    carry = lax.fori_loop(0, n_full, functools.partial(step, masked=False), carry)
    top, acc = lax.fori_loop(n_full, n_all, functools.partial(step, masked=True), carry)
    total = acc[HD : HD + 1]
    out = acc[:HD] / total
    low = bf(out)
    rest = bf(out - f32(low))
    for h in range(heads):
        o_ref[HD * h : HD * (h + 1), :] = low[:, h * bq : (h + 1) * bq]
        rest_ref[HD * h : HD * (h + 1), :] = rest[:, h * bq : (h + 1) * bq]
    lse_ref[...] = (top + jnp.log(total)).reshape(lse_ref.shape)


def attn_fwd(info, q, loc, rem, bq, bk):
    group, length = q.shape
    blocks = length // bq
    width = group // HD * bq
    return pl.pallas_call(
        functools.partial(attn_fwd_kernel, bk),
        grid=(blocks,),
        in_specs=[
            pl.BlockSpec(memory_space=pltpu.SMEM),
            pl.BlockSpec((group, bq), lambda i: (0, i)),
            whole(),
            whole(),
        ],
        out_specs=[
            pl.BlockSpec((group, bq), lambda i: (0, i)),
            pl.BlockSpec((group, bq), lambda i: (0, i)),
            pl.BlockSpec((1, 1, width), lambda i: (i, 0, 0)),
        ],
        out_shape=[
            jax.ShapeDtypeStruct((group, length), BF16),
            jax.ShapeDtypeStruct((group, length), BF16),
            jax.ShapeDtypeStruct((blocks, 1, width), F32),
        ],
        scratch_shapes=[
            pltpu.VMEM((2 * length // bk, bk, HD), BF16),
            pltpu.VMEM((2 * length // bk, HD + 16, bk), BF16),
        ],
        compiler_params=pltpu.CompilerParams(vmem_limit_bytes=VMEM_CAP),
        cost_estimate=pl.CostEstimate(flops=16 * group * length * length, bytes_accessed=8 * group * length, transcendentals=group * length * length // HD),
        name="attention",
    )(info, q, loc, rem)


def attn_bwd_kernel(bk, info_ref, q_ref, do_ref, o_ref, rest_ref, lse_ref, loc_ref, rem_ref, rope_q, rope_l, rope_r,
                    dq_ref, dloc_ref, drem_ref, sum_ref, k3, kt3, v3, dk3, dv3):
    qi = pl.program_id(0)
    length = loc_ref.shape[1]
    blocks = length // bk
    heads = q_ref.shape[0] // HD
    bq = q_ref.shape[1]
    hd = HD // 2

    @pl.when(qi == 0)
    def _():
        for side, ref in enumerate((loc_ref, rem_ref)):
            for b in range(blocks):
                cols = slice(b * bk, (b + 1) * bk)
                k3[side * blocks + b] = jnp.transpose(ref[:HD, cols])
                kt3[side * blocks + b] = ref[:HD, cols]
                v3[side * blocks + b] = jnp.transpose(ref[HD:, cols])
        dk3[...] = jnp.zeros_like(dk3)
        dv3[...] = jnp.zeros_like(dv3)

    first, n_full, n_all, starts = spans(info_ref, qi, bq, bk, length)
    q = stack_heads(q_ref, heads)
    do = stack_heads(do_ref, heads)
    o = f32(stack_heads(o_ref, heads)) + f32(stack_heads(rest_ref, heads))
    delta = jnp.sum(f32(do) * o, axis=0, keepdims=True)
    lse = lse_ref[...].reshape(1, heads * bq)
    shift = info_ref[0] * blocks

    def step(b, dq, masked):
        slot = lax.rem(b + shift, 2 * blocks)
        s = nn(k3[slot], q)
        if masked:
            ok = allowed_tile(first, b * bk, starts, bk, bq)
            s = jnp.concatenate([jnp.where(ok, s[:, h * bq : (h + 1) * bq], neg_fill) for h in range(heads)], axis=1)
        p = jnp.exp(s - lse)
        dp = nn(v3[slot], do)
        ds = bf(p * (dp - delta))
        dv3[slot] += nt(do, bf(p))
        dk3[slot] += nt(q, ds)
        return dq + nn(kt3[slot], ds)

    dq = jnp.zeros((HD, heads * bq), F32)
    dq = lax.fori_loop(0, n_full, functools.partial(step, masked=False), dq)
    dq = lax.fori_loop(n_full, n_all, functools.partial(step, masked=True), dq)

    def back(v, table):
        cos, sin = table[:hd], table[hd:]
        a, b = v[:hd], v[hd:]
        return jnp.concatenate([a * cos + b * sin, b * cos - a * sin], axis=0)

    scale = HD**-0.5
    table = rope_q[...]
    for h in range(heads):
        dq_ref[HD * h : HD * (h + 1), :] = bf(back(dq[:, h * bq : (h + 1) * bq] * scale, table))

    @pl.when(qi == pl.num_programs(0) - 1)
    def _():
        fold = jnp.zeros(sum_ref.shape, F32)
        for side, (ref, rope) in enumerate(((dloc_ref, rope_l), (drem_ref, rope_r))):
            for b in range(blocks):
                cols = slice(b * bk, (b + 1) * bk)
                both = jnp.concatenate([back(dk3[side * blocks + b], rope[:, cols]), dv3[side * blocks + b]], axis=0)
                ref[:, cols] = both.astype(ref.dtype)
                for o in range(0, bk, LANES):
                    fold = fold + both[:, o : o + LANES]
        sum_ref[...] = fold


def attn_bwd(info, q, do, o, rest, lse, loc, rem, rope_loc, rope_rem, bq, bk):
    group, length = q.shape
    blocks = length // bq
    width = group // HD * bq
    rows = pl.BlockSpec((group, bq), lambda i: (0, i))
    return pl.pallas_call(
        functools.partial(attn_bwd_kernel, bk),
        grid=(blocks,),
        in_specs=[
            pl.BlockSpec(memory_space=pltpu.SMEM),
            rows, rows, rows, rows,
            pl.BlockSpec((1, 1, width), lambda i: (i, 0, 0)),
            whole(), whole(),
            pl.BlockSpec((HD, bq), lambda i: (0, i)),
            whole(), whole(),
        ],
        out_specs=[rows, whole(), whole(), whole()],
        out_shape=[
            jax.ShapeDtypeStruct((group, length), BF16),
            jax.ShapeDtypeStruct(loc.shape, F32),
            jax.ShapeDtypeStruct(loc.shape, BF16),
            jax.ShapeDtypeStruct((loc.shape[0], LANES), F32),
        ],
        scratch_shapes=[
            pltpu.VMEM((2 * length // bk, bk, HD), BF16),
            pltpu.VMEM((2 * length // bk, HD, bk), BF16),
            pltpu.VMEM((2 * length // bk, bk, HD), BF16),
            pltpu.VMEM((2 * length // bk, HD, bk), F32),
            pltpu.VMEM((2 * length // bk, HD, bk), F32),
        ],
        compiler_params=pltpu.CompilerParams(vmem_limit_bytes=VMEM_CAP),
        cost_estimate=pl.CostEstimate(flops=40 * group * length * length, bytes_accessed=16 * group * length, transcendentals=group * length * length // HD),
        name="attention_back",
    )(info, q, do, o, rest, lse, loc, rem, rope_loc, rope_loc, rope_rem)


def rope_table(first, length):
    half = HD // 2
    inverse = rope_base ** (-(jnp.arange(half).astype(F32) * 2.0 / HD))
    angles = inverse[:, None] * f32(first + jnp.arange(length, dtype=jnp.int32))[None, :]
    return jnp.concatenate([jnp.cos(angles), jnp.sin(angles)], axis=0)


def rope(v, table):
    half = HD // 2
    shaped = v.reshape(-1, 2, half, v.shape[1])
    cos, sin = table[None, :half], table[None, half:]
    a, b = shaped[:, 0], shaped[:, 1]
    return jnp.stack([a * cos - b * sin, b * cos + a * sin], axis=1).reshape(v.shape)


def device_order(rows, count):
    p = jnp.arange(8 * count * rows, dtype=jnp.int32)
    q = p // (count * 2 * rows)
    z = (p // (2 * rows)) % count
    c = (p // rows) % 2
    x_rel = ((q == 1) | (q == 3)).astype(jnp.int32)
    y_rel = (q >= 2).astype(jnp.int32)
    chip = z * 2 + (lax.axis_index("xx") ^ x_rel)
    flat = (chip * 2 + c) * 2 + (lax.axis_index("ctx") ^ y_rel)
    return flat * rows + p % rows


def column(v, rows):
    return jnp.pad(v, (0, rows - v.shape[0]))[:, None]


def shards(
    tokens, image_starts, attn_gain, query_weight, query_bias, key_weight, key_bias, value_weight, value_bias,
    out_weight, mlp_gain, gate_weight, up_weight, down_weight, cotangent,
):
    length, width = tokens.shape
    count = lax.axis_size("zz")
    devices = 8 * count
    rows = width // devices
    core = lax.axis_index("core")
    ctx = lax.axis_index("ctx")
    core_arr = core.reshape(1).astype(jnp.int32)
    feat = query_weight.shape[1]
    kv_feat = key_weight.shape[1]
    ff = gate_weight.shape[1]
    half_ff = ff // 2
    units = half_ff // LANES
    cuts = [0, units // 5 * 2 + 2, units]
    chunks = tuple((a * LANES, (b - a) * LANES) for a, b in zip(cuts, cuts[1:]))
    n = len(chunks)
    own_first = core == 0

    extras = jnp.concatenate(
        [column(v, rows) for v in (attn_gain, mlp_gain, query_bias, key_bias, value_bias)]
        + [jnp.zeros((rows, EXTRA - 5), BF16)], axis=1)
    fh, kh = feat // 2, kv_feat // 2
    sides = [
        jnp.concatenate([query_weight[:, s * fh : (s + 1) * fh], key_weight[:, s * kh : (s + 1) * kh],
                         value_weight[:, s * kh : (s + 1) * kh], out_weight[:, s * fh : (s + 1) * fh], extras], axis=1)
        for s in range(2)
    ]
    a_own = pair_rows(jnp.where(own_first, sides[0], sides[1]), jnp.where(own_first, sides[1], sides[0]))
    tokens, cotangent = after((tokens, cotangent), a_own)
    a_zs = along_z(a_own, True)
    gate_weight, up_weight, down_weight = after((gate_weight, up_weight, down_weight), a_own)
    packed = pack(core_arr, gate_weight, up_weight, down_weight, chunks)
    own = [pair_rows(packed[i], packed[n + i]) for i in range(n)]
    f_zs = [along_z(v, False) for v in own]

    natural = device_order(rows, count)
    to_dev = bf(jnp.arange(width, dtype=jnp.int32)[:, None] == natural[None, :])
    x = nn(tokens, to_dev)
    r1 = lax.rsqrt(jnp.mean(x * x, axis=-1, keepdims=True) + eps)
    table = rope_table(ctx * length, length)
    table_rem = rope_table((1 - ctx) * length, length)

    a_xs, a_ys = beside(a_zs)
    a_pieces = [a_zs, a_xs, a_ys, *diagonal(a_xs, a_ys)]
    w_mine = jnp.concatenate(a_pieces, axis=0)
    w_side = [w_mine, swap(w_mine, "core")]

    q0, k0, v0, o0, e0 = 0, fh, fh + kh, fh + 2 * kh, 2 * fh + 2 * kh
    extra_rel = w_mine[:, e0:]
    gains = jnp.transpose(f32(extra_rel[:, :2]))
    gain_attn, gain_mlp = gains[0:1], gains[1:2]
    bias_nat = nn(to_dev, extra_rel)
    q_bias = bias_nat[:, 2]
    kv_rows = kv_feat // devices
    k_bias = bias_nat[:, 3].reshape(devices, rows)[:, :kv_rows].reshape(-1)
    v_bias = bias_nat[:, 4].reshape(devices, rows)[:, :kv_rows].reshape(-1)

    def by_side(v):
        lo, hi = v[: v.shape[0] // 2], v[v.shape[0] // 2 :]
        return jnp.where(own_first, lo, hi), jnp.where(own_first, hi, lo)

    normed_one = bf(x * r1 * gain_attn)
    keys_values = []
    for w_all, kb, vb in zip(w_side, by_side(k_bias), by_side(v_bias)):
        kv = lax.dot_general(w_all[:, k0:o0], normed_one, (((0,), (1,)), ((), ())), preferred_element_type=F32)
        kv = kv + jnp.concatenate([kb, vb])[:, None]
        keys_values.append(jnp.concatenate([bf(rope(kv[:kh], table)), bf(kv[kh:])], axis=0))
    kv_rem = swap(jnp.concatenate(keys_values, axis=0), "ctx")
    kv_rem = [kv_rem[: 2 * kh], kv_rem[2 * kh :]]
    queries = []
    for w_all, qb in zip(w_side, by_side(q_bias)):
        q = lax.dot_general(w_all[:, :k0], after(normed_one, *keys_values), (((0,), (1,)), ((), ())), preferred_element_type=F32)
        queries.append(bf(rope(q + qb[:, None], table) * HD**-0.5))
    f_xy = [None] * n
    f_diag = [None] * n
    f_xs = swap(after(f_zs[0], normed_one), "xx")
    f_ys = swap(after(f_zs[0], *kv_rem), "ctx")
    f_xy[0] = (f_xs, f_ys)

    info = jnp.concatenate([ctx.reshape(1).astype(jnp.int32), image_starts[0]])
    bq = min(256, length)
    bk = min(256, length)
    queries[0] = after(queries[0], f_zs[0])
    att0, rest0, lse0 = attn_fwd(info, queries[0], keys_values[0], kv_rem[0], bq, bk)
    f_xy[0] = after(f_xy[0], att0)
    f_diag[0] = diagonal(*f_xy[0])
    f_zs[1] = after(f_zs[1], att0)
    f_xy[1] = beside(f_zs[1])
    queries[1] = after(queries[1], f_xy[0], f_zs[1])
    att1, rest1, lse1 = attn_fwd(info, queries[1], keys_values[1], kv_rem[1], bq, bk)
    f_xy[1] = after(f_xy[1], att1)
    f_diag[1] = diagonal(*f_xy[1])
    for i in range(2, n):
        f_zs[i] = after(f_zs[i], att1)
        f_xy[i] = beside(f_zs[i])
    attended, rest, lse = [att0, att1], [rest0, rest1], [lse0, lse1]

    cotangent = after(cotangent, att0)
    cot = bf(nn(cotangent, to_dev))
    cot_theirs = swap(cot, "core")
    hidden = x
    for a, w_all in zip(attended, w_side):
        hidden = hidden + lax.dot_general(a, w_all[:, o0:e0], (((0,), (1,)), ((), ())), preferred_element_type=F32)
    r2 = lax.rsqrt(jnp.mean(hidden * hidden, axis=-1, keepdims=True) + eps)
    normed_two = bf(hidden * r2 * gain_mlp)
    normed_theirs = swap(normed_two, "core")

    results, got_d, got_b, got_z = [], [None] * n, [None] * n, [None] * n
    x_in = normed_two
    for i in range(n):
        r = mlp(x_in, normed_theirs, cot, cot_theirs, [f_zs[i], *f_xy[i], *f_diag[i]])
        results.append(r)
        x_in = after(normed_two, r[2])
        if i + 2 < n:
            f_xy[i + 2] = after(f_xy[i + 2], r[2])
            f_diag[i + 2] = diagonal(*f_xy[i + 2])
        got_d[i] = sum_diagonal(r[4:])
        if i > 0:
            got_d[i - 1] = after(got_d[i - 1], r[2])
            got_b[i - 1] = sum_beside(results[i - 1][4:], got_d[i - 1])

    def total(a, b):
        mine = sum(f32(r[a]) for r in results)
        return mine + f32(swap(bf(sum(f32(r[b]) for r in results)), "core"))

    grad_two = total(2, 3)
    mlp_gain_grad = jnp.sum(grad_two * hidden * r2, axis=0)
    u = grad_two * gain_mlp
    grad_hidden = f32(cot) + r2 * u - hidden * (r2 * r2 * r2) * jnp.mean(u * hidden, axis=-1, keepdims=True)
    grad_attn = bf(grad_hidden)
    grad_mixed = [
        bf(lax.dot_general(w_all[:, o0:e0], grad_attn, (((0,), (1,)), ((), ())), preferred_element_type=F32)) for w_all in w_side
    ]

    back = [None, None]
    lows, kv_got = [], [None, None]
    for s in range(2):
        do = grad_mixed[s]
        if s == 1:
            zs = []
            for i in range(n - 1):
                zs.append(sum_own(results[i][4:], after(got_b[i], back[0][0])))
                got_z[i] = sum_along_z(zs[i], False)
            got_d[n - 1] = after(got_d[n - 1], back[0][0])
            got_b[n - 1] = sum_beside(results[n - 1][4:], got_d[n - 1])
            do = after(do, back[0][0], *zs)
        back[s] = attn_bwd(info, queries[s], do, attended[s], rest[s], lse[s], keys_values[s], kv_rem[s], table, table_rem, bq, bk)
        kv_got[s] = swap(back[s][2], "ctx")
    zs_last = sum_own(results[n - 1][4:], after(got_b[n - 1], back[1][0]))
    got_z[n - 1] = sum_along_z(zs_last, False)
    back[1] = after(back[1], zs_last)
    for s in range(2):
        query_low, d_loc, d_rem, _ = back[s]
        kv_low = bf(d_loc + f32(kv_got[s]))
        lows.append(jnp.concatenate([query_low, kv_low], axis=0))

    out_sum = total(0, 1)
    output = bf(nt(bf(hidden + out_sum), to_dev))
    mlp_out = [sum_pair(z) for z in got_z]
    gate_grad, up_grad, down_grad = unpack(core_arr, [m[0] for m in mlp_out], [m[1] for m in mlp_out], chunks, ff)

    out_grad = [lax.dot_general(grad_attn, a, (((0,), (1,)), ((), ())), preferred_element_type=F32) for a in attended]
    grad_one = 0.0
    for low, w_all in zip(lows, w_side):
        grad_one = grad_one + lax.dot_general(low, w_all[:, :o0], (((0,), (1,)), ((), ())), preferred_element_type=F32)
    w = grad_one * gain_attn
    tokens_grad_dev = grad_hidden + r1 * w - x * (r1 * r1 * r1) * jnp.mean(w * x, axis=-1, keepdims=True)
    tokens_grad = bf(nt(bf(tokens_grad_dev), to_dev))
    attn_gain_grad = jnp.sum(grad_one * x * r1, axis=0)
    qkv_grad = [lax.dot_general(normed_one, low, (((0,), (1,)), ((), ())), preferred_element_type=F32) for low in lows]
    bias_grad = [jnp.concatenate([jnp.sum(f32(b[0]), axis=1), jnp.sum(b[3], axis=1)]) for b in back]

    def whole_order(a, b):
        return jnp.where(own_first, jnp.concatenate([a, b]), jnp.concatenate([b, a]))

    def spread(v):
        return jnp.pad(v.reshape(devices, -1), ((0, 0), (0, rows - v.shape[0] // devices))).reshape(-1)

    qb, kb, vb = [whole_order(bias_grad[0][a:b], bias_grad[1][a:b]) for a, b in ((q0, k0), (k0, v0), (v0, o0))]
    nat_cols = jnp.stack([qb, spread(kb), spread(vb)], axis=0)
    dev_cols = nn(two_parts(nat_cols.T).T, to_dev)
    dev_cols = dev_cols[:3] + dev_cols[3:]
    vec_cols = jnp.concatenate([attn_gain_grad[None], mlp_gain_grad[None], dev_cols, jnp.zeros((EXTRA // 2 - 5, width), F32)], axis=0)
    extra_grad = two_parts(jnp.transpose(vec_cols))
    g_mine = jnp.concatenate([bf(qkv_grad[0]), bf(out_grad[0]), extra_grad], axis=1)
    g_theirs = jnp.concatenate([bf(qkv_grad[1]), bf(out_grad[1])], axis=1)
    got = swap(g_theirs, "core")
    g_sum = jnp.concatenate([bf(f32(g_mine[:, :e0]) + f32(got)), g_mine[:, e0:]], axis=1)
    quarter = width // 4
    bounds = [0, quarter, 2 * quarter, 3 * quarter, 3 * quarter + quarter // 2, width]
    g_pieces = [g_sum[a:b] for a, b in zip(bounds, bounds[1:])]
    g_got = sum_beside(g_pieces, sum_diagonal(g_pieces), EXTRA)
    a_mine, a_theirs = sum_pair(sum_along_z(sum_own(g_pieces, g_got, EXTRA), True))

    def natural_cols(a, b):
        lo, hi = a_mine[:, a:b], a_theirs[:, a:b]
        return jnp.where(own_first, jnp.concatenate([lo, hi], axis=1), jnp.concatenate([hi, lo], axis=1))

    extra = a_mine[:, e0:] + a_theirs[:, e0:]
    extra = extra[:, : EXTRA // 2] + extra[:, EXTRA // 2 :]
    return (
        output,
        tokens_grad,
        extra[:, 0],
        natural_cols(q0, k0),
        extra[:, 2],
        natural_cols(k0, v0),
        extra[:kv_rows, 3],
        natural_cols(v0, o0),
        extra[:kv_rows, 4],
        natural_cols(o0, e0),
        extra[:, 1],
        gate_grad,
        up_grad,
        down_grad,
    )


def solution(mesh):
    dp, ctx = mesh.devices.shape
    fine = Mesh(mesh.devices.reshape(dp // 4, 2, 2, ctx), ("zz", "xx", "core", "ctx"))
    every = ("zz", "xx", "core", "ctx")
    mat, vec = P(every, None), P(every)
    placed = (mat, P(("zz", "xx", "core"), None), vec, mat, vec, mat, vec, mat, vec, mat, vec, mat, mat, mat, mat)
    outs = (mat, mat, vec, mat, vec, mat, vec, mat, vec, mat, vec, mat, mat, mat)
    return jax.shard_map(shards, mesh=fine, in_specs=placed, out_specs=outs, check_vma=False)
```

```python
import functools

import jax
import jax.numpy as jnp
from jax import lax
from jax.experimental import pallas as pl
from jax.experimental.pallas import tpu as pltpu
from jax.sharding import Mesh, PartitionSpec as P

HD = 64
IMG = 256
KV_HEADS = 2
LANES = 128
EXTRA = 128
TILE = 256

eps = 1e-06
rope_base = 1000000.0
neg_fill = -1e30

SWAP = ((0, 1), (1, 0))
F32 = jnp.float32
BF16 = jnp.bfloat16
VMEM_CAP = 60 * 1024 * 1024


def f32(v):
    return v.astype(F32)


def bf(v):
    return v.astype(BF16)


def nn(a, b):
    return jnp.dot(a, b, preferred_element_type=F32)


def nt(a, b):
    return lax.dot_general(a, b, (((1,), (1,)), ((), ())), preferred_element_type=F32)


def tn(a, b):
    return lax.dot_general(a, b, (((0,), (0,)), ((), ())), preferred_element_type=F32)


def swap(v, axis):
    return lax.ppermute(v, axis, SWAP)


def whole():
    return pl.BlockSpec(memory_space=pltpu.VMEM)


def after(values, *earlier):
    return lax.optimization_barrier((values, earlier))[0]


def along_z(own, direct):
    count = lax.axis_size("zz")
    if not direct:
        return lax.all_gather(own, "zz", axis=0, tiled=True)
    rows = own.shape[0]
    me = lax.axis_index("zz")
    zs = jnp.zeros((count * rows, own.shape[1]), own.dtype)
    zs = lax.dynamic_update_slice(zs, own, (me * rows, 0))
    for j in range(1, count):
        got = lax.ppermute(own, "zz", [(i, i ^ j) for i in range(count)])
        zs = lax.dynamic_update_slice(zs, got, ((me ^ j) * rows, 0))
    return zs


def beside(zs):
    return swap(zs, "xx"), swap(zs, "ctx")


def diagonal(xs, ys):
    half = xs.shape[0] // 2
    return swap(ys[:half], "xx"), swap(xs[half:], "ctx")


def sum_diagonal(pieces):
    return swap(pieces[3], "xx"), swap(pieces[4], "ctx")


def two_parts(v):
    high = lax.optimization_barrier(bf(v))
    return jnp.concatenate([high, bf(v - f32(high))], axis=1)


def rounded(v, vectors):
    if not vectors:
        return bf(v)
    tail = v[:, -vectors:]
    half = vectors // 2
    return jnp.concatenate([bf(v[:, :-vectors]), two_parts(tail[:, :half] + tail[:, half:])], axis=1)


def sum_beside(pieces, got, vectors=0):
    half = pieces[3].shape[0]
    xs = rounded(f32(pieces[1]) + jnp.pad(f32(got[1]), ((half, 0), (0, 0))), vectors)
    ys = rounded(f32(pieces[2]) + jnp.pad(f32(got[0]), ((0, half), (0, 0))), vectors)
    return swap(xs, "xx"), swap(ys, "ctx")


def sum_own(pieces, got, vectors=0):
    return rounded(f32(pieces[0]) + f32(got[0]) + f32(got[1]), vectors)


def sum_along_z(zs, direct):
    count = lax.axis_size("zz")
    me = lax.axis_index("zz")
    if not direct:
        return [lax.optimization_barrier(lax.psum_scatter(zs, "zz", scatter_dimension=0, tiled=True))]
    rows = zs.shape[0] // count
    parts = [lax.dynamic_slice(zs, (me * rows, 0), (rows, zs.shape[1]))]
    for j in range(1, count):
        part = lax.dynamic_slice(zs, ((me ^ j) * rows, 0), (rows, zs.shape[1]))
        parts.append(lax.ppermute(part, "zz", [(i, i ^ j) for i in range(count)]))
    return parts


def sum_pair(parts):
    own = sum(f32(p) for p in parts)
    rows = own.shape[0]
    first, second = own[: rows // 2], own[rows // 2 :]
    here = lax.axis_index("core") == 0
    return jnp.where(here, first, second), swap(jnp.where(here, second, first), "core")


def pair_rows(mine, theirs):
    got = swap(theirs, "core")
    here = lax.axis_index("core") == 0
    return jnp.where(here, jnp.concatenate([mine, got], axis=0), jnp.concatenate([got, mine], axis=0))


def tiles_of(width):
    return [(o, min(TILE, width - o)) for o in range(0, width, TILE)]


def pack_kernel(chunks, core_ref, gate_ref, up_ref, down_ref, *outs):
    core = core_ref[0]
    half = gate_ref.shape[1] // 2
    for side in range(2):
        base = jnp.where(side == 0, core, 1 - core) * half
        for (start, width), out in zip(chunks, outs[side * len(chunks) : (side + 1) * len(chunks)]):
            for o, t in tiles_of(width):
                for k, ref in enumerate((gate_ref, up_ref, down_ref)):
                    at = pl.multiple_of(base + (start + o), LANES)
                    out[:, 3 * o + k * t : 3 * o + (k + 1) * t] = ref[:, pl.ds(at, t)]


def pack(core, gate, up, down, chunks):
    rows = gate.shape[0]
    shapes = [jax.ShapeDtypeStruct((rows, 3 * w), gate.dtype) for _, w in chunks] * 2
    return pl.pallas_call(
        functools.partial(pack_kernel, chunks),
        in_specs=[pl.BlockSpec(memory_space=pltpu.SMEM)] + [whole()] * 3,
        out_specs=[whole()] * len(shapes),
        out_shape=shapes,
        name="pack",
    )(core, gate, up, down)


def pack_attn_kernel(core_ref, q_ref, k_ref, v_ref, o_ref, vec_ref, mine_ref, theirs_ref):
    rows = q_ref.shape[0]
    fh, kh = q_ref.shape[1] // 2, k_ref.shape[1] // 2

    def side(s, out):
        out[...] = jnp.concatenate(
            [q_ref[:, s * fh : (s + 1) * fh], k_ref[:, s * kh : (s + 1) * kh], v_ref[:, s * kh : (s + 1) * kh],
             o_ref[:, s * fh : (s + 1) * fh], vec_ref[...]], axis=1)

    @pl.when(core_ref[0] == 0)
    def _():
        side(0, mine_ref)
        side(1, theirs_ref)

    @pl.when(core_ref[0] != 0)
    def _():
        side(1, mine_ref)
        side(0, theirs_ref)


def pack_attn(core, q, k, v, o, vec):
    shape = jax.ShapeDtypeStruct((q.shape[0], (q.shape[1] + k.shape[1] + v.shape[1] + o.shape[1]) // 2 + vec.shape[1]), q.dtype)
    return pl.pallas_call(
        pack_attn_kernel,
        in_specs=[pl.BlockSpec(memory_space=pltpu.SMEM)] + [whole()] * 5,
        out_specs=[whole()] * 2,
        out_shape=[shape] * 2,
        name="pack_attention",
    )(core, q, k, v, o, vec)


def unpack_kernel(chunks, core_ref, *refs):
    core = core_ref[0]
    ins, outs = refs[: 2 * len(chunks)], refs[2 * len(chunks) :]
    half = outs[0].shape[1] // 2
    for side in range(2):
        base = jnp.where(side == 0, core, 1 - core) * half
        for (start, width), ref in zip(chunks, ins[side * len(chunks) : (side + 1) * len(chunks)]):
            for o, t in tiles_of(width):
                for k, out in enumerate(outs):
                    at = pl.multiple_of(base + (start + o), LANES)
                    out[:, pl.ds(at, t)] = ref[:, 3 * o + k * t : 3 * o + (k + 1) * t]


def unpack(core, mine, theirs, chunks, width):
    rows = mine[0].shape[0]
    shapes = [jax.ShapeDtypeStruct((rows, width), F32)] * 3
    return pl.pallas_call(
        functools.partial(unpack_kernel, chunks),
        in_specs=[pl.BlockSpec(memory_space=pltpu.SMEM)] + [whole()] * (2 * len(chunks)),
        out_specs=[whole()] * 3,
        out_shape=shapes,
        name="unpack",
    )(core, *mine, *theirs)


def mlp_kernel(last_t, rows, xm, xt, cm, ct, zw, xw, yw, aw, bw, om, ot, gm, gt, dz, dx, dy, da, db,
               xs, cs, oacc, gacc, w, h, low, sem):
    step = pl.program_id(0)
    steps = pl.num_programs(0)
    tokens = xm.shape[0]
    quarter = zw.shape[0]
    half = quarter // 2

    @pl.when(step == 0)
    def _():
        copies = [
            pltpu.make_async_copy(src, dst.at[pl.ds(o, tokens)], sem.at[i])
            for i, (src, dst, o) in enumerate(((xm, xs, 0), (xt, xs, tokens), (cm, cs, 0), (ct, cs, tokens)))
        ]
        for c in copies:
            c.start()
        for c in copies:
            c.wait()

    w[0:quarter] = zw[...]
    w[quarter : 2 * quarter] = xw[...]
    w[2 * quarter : 3 * quarter] = yw[...]
    w[3 * quarter : 3 * quarter + half] = aw[...]
    w[3 * quarter + half :] = bw[...]

    def grads(t):
        for x_ref, a, b in ((xs, 0, t), (xs, t, 2 * t), (cs, 2 * t, 3 * t)):
            d = bf(tn(x_ref[...], h[:, a:b]))
            dz[:, a:b] = d[:quarter]
            dx[:, a:b] = d[quarter : 2 * quarter]
            dy[:, a:b] = d[2 * quarter : 3 * quarter]
            da[:, a:b] = d[3 * quarter : 3 * quarter + half]
            db[:, a:b] = d[3 * quarter + half :]

    def work(t):
        def block(i, carry):
            at = pl.multiple_of(i * rows, rows)
            here = pl.ds(at, rows)
            x = xs[here, :]
            g = nn(x, w[:, :t])
            u = nn(x, w[:, t : 2 * t])
            ga = nn(cs[here, :], w[:, 2 * t : 3 * t])
            sg = 0.5 * jnp.tanh(0.5 * g) + 0.5
            silu = g * sg
            h[here, 2 * t : 3 * t] = bf(silu * u)
            h[here, :t] = bf(ga * u * (sg + silu * (1.0 - sg)))
            h[here, t : 2 * t] = bf(ga * silu)
            old = step > 0
            o = nt(h[here, 2 * t : 3 * t], w[:, 2 * t : 3 * t])
            oacc[here, :] = o + jnp.where(old, oacc[here, :], 0.0)
            gn = nt(h[here, : 2 * t], w[:, : 2 * t])
            gacc[here, :] = gn + jnp.where(old, gacc[here, :], 0.0)
            return carry

        lax.fori_loop(0, 2 * tokens // rows, block, 0)

    def sums_out():
        return [
            pltpu.make_async_copy(low.at[i], dst, sem.at[i])
            for i, dst in enumerate((gt, gm, ot, om))
        ]

    def tile(t):
        work(t)

        @pl.when(step == steps - 1)
        def _():
            for i, (acc, part) in enumerate(((gacc, 1), (gacc, 0), (oacc, 1), (oacc, 0))):
                low[i] = bf(acc[pl.ds(part * tokens, tokens), :])
            for c in sums_out():
                c.start()

        grads(t)

    if last_t == TILE:
        tile(TILE)
    else:
        @pl.when(step < steps - 1)
        def _():
            tile(TILE)

        @pl.when(step == steps - 1)
        def _():
            tile(last_t)

    @pl.when(step == steps - 1)
    def _():
        for c in sums_out():
            c.wait()


def mlp(xm, xt, cm, ct, pieces, rows=1024):
    tokens, width = xm.shape
    cols = pieces[0].shape[1] // 3
    steps = pl.cdiv(cols, TILE)
    last_t = cols - (steps - 1) * TILE
    block = lambda p: pl.BlockSpec((p.shape[0], 3 * TILE), lambda i: (0, i))
    any_space = pl.BlockSpec(memory_space=pl.ANY)
    lo = jax.ShapeDtypeStruct((tokens, width), BF16)
    return pl.pallas_call(
        functools.partial(mlp_kernel, last_t, rows),
        grid=(steps,),
        in_specs=[any_space] * 4 + [block(p) for p in pieces],
        out_specs=[any_space] * 4 + [block(p) for p in pieces],
        out_shape=[lo] * 4 + [jax.ShapeDtypeStruct(p.shape, BF16) for p in pieces],
        scratch_shapes=[
            pltpu.VMEM((2 * tokens, width), BF16),
            pltpu.VMEM((2 * tokens, width), BF16),
            pltpu.VMEM((2 * tokens, width), F32),
            pltpu.VMEM((2 * tokens, width), F32),
            pltpu.VMEM((width, 3 * TILE), BF16),
            pltpu.VMEM((2 * tokens, 3 * TILE), BF16),
            pltpu.VMEM((4, tokens, width), BF16),
            pltpu.SemaphoreType.DMA((4,)),
        ],
        compiler_params=pltpu.CompilerParams(vmem_limit_bytes=VMEM_CAP),
        cost_estimate=pl.CostEstimate(flops=9 * 2 * 2 * tokens * width * cols, bytes_accessed=12 * width * cols, transcendentals=0),
        name="feed_forward",
    )(xm, xt, cm, ct, *pieces)


def spans(info_ref, qi, bq, bk, length):
    first = info_ref[0] * length + qi * bq
    last = first + bq - 1
    top = last + 1
    starts = (info_ref[1], info_ref[2])
    for s in starts:
        top = jnp.where((s <= last) & (s + IMG > first), jnp.maximum(top, s + IMG), top)
    return first, (first + 1) // bk, (top + bk - 1) // bk, starts


def allowed_tile(first, key_first, starts, bk, bq):
    kp = key_first + lax.broadcasted_iota(jnp.int32, (bk, bq), 0)
    qp = first + lax.broadcasted_iota(jnp.int32, (bk, bq), 1)
    ok = kp <= qp
    for s in starts:
        ok = ok | ((kp >= s) & (kp < s + IMG) & (qp >= s) & (qp < s + IMG))
    return ok


def stack_heads(ref, heads):
    return jnp.concatenate([ref[HD * h : HD * (h + 1), :] for h in range(heads)], axis=1)


def attn_fwd_kernel(bk, info_ref, q_ref, loc_ref, rem_ref, o_ref, rest_ref, lse_ref, k3, vt3):
    qi = pl.program_id(0)
    length = loc_ref.shape[1]
    blocks = length // bk
    heads = q_ref.shape[0] // HD
    bq = q_ref.shape[1]

    @pl.when(qi == 0)
    def _():
        for side, ref in enumerate((loc_ref, rem_ref)):
            for b in range(blocks):
                cols = slice(b * bk, (b + 1) * bk)
                k3[side * blocks + b] = jnp.transpose(ref[:HD, cols])
                vt3[side * blocks + b, :HD] = ref[HD:, cols]
                vt3[side * blocks + b, HD:] = jnp.ones((16, bk), BF16)

    first, n_full, n_all, starts = spans(info_ref, qi, bq, bk, length)
    q = stack_heads(q_ref, heads)
    width = heads * bq
    shift = info_ref[0] * blocks

    def step(b, carry, masked):
        top, acc = carry
        slot = lax.rem(b + shift, 2 * blocks)
        s = nn(k3[slot], q)
        if masked:
            ok = allowed_tile(first, b * bk, starts, bk, bq)
            s = jnp.concatenate([jnp.where(ok, s[:, h * bq : (h + 1) * bq], neg_fill) for h in range(heads)], axis=1)
        new_top = jnp.maximum(top, jnp.max(s, axis=0, keepdims=True))
        p = jnp.exp(s - new_top)
        scale = jnp.exp(top - new_top)
        acc = acc * scale + nn(vt3[slot], bf(p))
        return new_top, acc

    carry = (jnp.full((1, width), neg_fill, F32), jnp.zeros((HD + 16, width), F32))
    carry = lax.fori_loop(0, n_full, functools.partial(step, masked=False), carry)
    top, acc = lax.fori_loop(n_full, n_all, functools.partial(step, masked=True), carry)
    total = acc[HD : HD + 1]
    out = acc[:HD] / total
    low = bf(out)
    rest = bf(out - f32(low))
    for h in range(heads):
        o_ref[HD * h : HD * (h + 1), :] = low[:, h * bq : (h + 1) * bq]
        rest_ref[HD * h : HD * (h + 1), :] = rest[:, h * bq : (h + 1) * bq]
    lse_ref[...] = (top + jnp.log(total)).reshape(lse_ref.shape)


def attn_fwd(info, q, loc, rem, bq, bk):
    group, length = q.shape
    blocks = length // bq
    width = group // HD * bq
    return pl.pallas_call(
        functools.partial(attn_fwd_kernel, bk),
        grid=(blocks,),
        in_specs=[
            pl.BlockSpec(memory_space=pltpu.SMEM),
            pl.BlockSpec((group, bq), lambda i: (0, i)),
            whole(),
            whole(),
        ],
        out_specs=[
            pl.BlockSpec((group, bq), lambda i: (0, i)),
            pl.BlockSpec((group, bq), lambda i: (0, i)),
            pl.BlockSpec((1, 1, width), lambda i: (i, 0, 0)),
        ],
        out_shape=[
            jax.ShapeDtypeStruct((group, length), BF16),
            jax.ShapeDtypeStruct((group, length), BF16),
            jax.ShapeDtypeStruct((blocks, 1, width), F32),
        ],
        scratch_shapes=[
            pltpu.VMEM((2 * length // bk, bk, HD), BF16),
            pltpu.VMEM((2 * length // bk, HD + 16, bk), BF16),
        ],
        compiler_params=pltpu.CompilerParams(vmem_limit_bytes=VMEM_CAP),
        cost_estimate=pl.CostEstimate(flops=16 * group * length * length, bytes_accessed=8 * group * length, transcendentals=group * length * length // HD),
        name="attention",
    )(info, q, loc, rem)


def attn_bwd_kernel(bk, info_ref, q_ref, do_ref, o_ref, rest_ref, lse_ref, loc_ref, rem_ref, rope_q, rope_l, rope_r,
                    dq_ref, dloc_ref, drem_ref, sum_ref, k3, kt3, v3, dk3, dv3):
    qi = pl.program_id(0)
    length = loc_ref.shape[1]
    blocks = length // bk
    heads = q_ref.shape[0] // HD
    bq = q_ref.shape[1]
    hd = HD // 2

    @pl.when(qi == 0)
    def _():
        for side, ref in enumerate((loc_ref, rem_ref)):
            for b in range(blocks):
                cols = slice(b * bk, (b + 1) * bk)
                k3[side * blocks + b] = jnp.transpose(ref[:HD, cols])
                kt3[side * blocks + b] = ref[:HD, cols]
                v3[side * blocks + b] = jnp.transpose(ref[HD:, cols])
        dk3[...] = jnp.zeros_like(dk3)
        dv3[...] = jnp.zeros_like(dv3)

    first, n_full, n_all, starts = spans(info_ref, qi, bq, bk, length)
    q = stack_heads(q_ref, heads)
    do = stack_heads(do_ref, heads)
    o = f32(stack_heads(o_ref, heads)) + f32(stack_heads(rest_ref, heads))
    delta = jnp.sum(f32(do) * o, axis=0, keepdims=True)
    lse = lse_ref[...].reshape(1, heads * bq)
    shift = info_ref[0] * blocks

    def step(b, dq, masked):
        slot = lax.rem(b + shift, 2 * blocks)
        s = nn(k3[slot], q)
        if masked:
            ok = allowed_tile(first, b * bk, starts, bk, bq)
            s = jnp.concatenate([jnp.where(ok, s[:, h * bq : (h + 1) * bq], neg_fill) for h in range(heads)], axis=1)
        p = jnp.exp(s - lse)
        dp = nn(v3[slot], do)
        ds = bf(p * (dp - delta))
        dv3[slot] += nt(do, bf(p))
        dk3[slot] += nt(q, ds)
        return dq + nn(kt3[slot], ds)

    dq = jnp.zeros((HD, heads * bq), F32)
    dq = lax.fori_loop(0, n_full, functools.partial(step, masked=False), dq)
    dq = lax.fori_loop(n_full, n_all, functools.partial(step, masked=True), dq)

    def back(v, table):
        cos, sin = table[:hd], table[hd:]
        a, b = v[:hd], v[hd:]
        return jnp.concatenate([a * cos + b * sin, b * cos - a * sin], axis=0)

    scale = HD**-0.5
    table = rope_q[...]
    for h in range(heads):
        dq_ref[HD * h : HD * (h + 1), :] = bf(back(dq[:, h * bq : (h + 1) * bq] * scale, table))

    @pl.when(qi == pl.num_programs(0) - 1)
    def _():
        fold = jnp.zeros(sum_ref.shape, F32)
        for side, (ref, rope) in enumerate(((dloc_ref, rope_l), (drem_ref, rope_r))):
            for b in range(blocks):
                cols = slice(b * bk, (b + 1) * bk)
                both = jnp.concatenate([back(dk3[side * blocks + b], rope[:, cols]), dv3[side * blocks + b]], axis=0)
                ref[:, cols] = both.astype(ref.dtype)
                for o in range(0, bk, LANES):
                    fold = fold + both[:, o : o + LANES]
        sum_ref[...] = fold


def attn_bwd(info, q, do, o, rest, lse, loc, rem, rope_loc, rope_rem, bq, bk):
    group, length = q.shape
    blocks = length // bq
    width = group // HD * bq
    rows = pl.BlockSpec((group, bq), lambda i: (0, i))
    return pl.pallas_call(
        functools.partial(attn_bwd_kernel, bk),
        grid=(blocks,),
        in_specs=[
            pl.BlockSpec(memory_space=pltpu.SMEM),
            rows, rows, rows, rows,
            pl.BlockSpec((1, 1, width), lambda i: (i, 0, 0)),
            whole(), whole(),
            pl.BlockSpec((HD, bq), lambda i: (0, i)),
            whole(), whole(),
        ],
        out_specs=[rows, whole(), whole(), whole()],
        out_shape=[
            jax.ShapeDtypeStruct((group, length), BF16),
            jax.ShapeDtypeStruct(loc.shape, F32),
            jax.ShapeDtypeStruct(loc.shape, BF16),
            jax.ShapeDtypeStruct((loc.shape[0], LANES), F32),
        ],
        scratch_shapes=[
            pltpu.VMEM((2 * length // bk, bk, HD), BF16),
            pltpu.VMEM((2 * length // bk, HD, bk), BF16),
            pltpu.VMEM((2 * length // bk, bk, HD), BF16),
            pltpu.VMEM((2 * length // bk, HD, bk), F32),
            pltpu.VMEM((2 * length // bk, HD, bk), F32),
        ],
        compiler_params=pltpu.CompilerParams(vmem_limit_bytes=VMEM_CAP),
        cost_estimate=pl.CostEstimate(flops=40 * group * length * length, bytes_accessed=16 * group * length, transcendentals=group * length * length // HD),
        name="attention_back",
    )(info, q, do, o, rest, lse, loc, rem, rope_loc, rope_loc, rope_rem)


def rope_table(first, length):
    half = HD // 2
    inverse = rope_base ** (-(jnp.arange(half).astype(F32) * 2.0 / HD))
    angles = inverse[:, None] * f32(first + jnp.arange(length, dtype=jnp.int32))[None, :]
    return jnp.concatenate([jnp.cos(angles), jnp.sin(angles)], axis=0)


def rope(v, table):
    half = HD // 2
    shaped = v.reshape(-1, 2, half, v.shape[1])
    cos, sin = table[None, :half], table[None, half:]
    a, b = shaped[:, 0], shaped[:, 1]
    return jnp.stack([a * cos - b * sin, b * cos + a * sin], axis=1).reshape(v.shape)


def device_order(rows, count):
    p = jnp.arange(8 * count * rows, dtype=jnp.int32)
    q = p // (count * 2 * rows)
    z = (p // (2 * rows)) % count
    c = (p // rows) % 2
    x_rel = ((q == 1) | (q == 3)).astype(jnp.int32)
    y_rel = (q >= 2).astype(jnp.int32)
    chip = z * 2 + (lax.axis_index("xx") ^ x_rel)
    flat = (chip * 2 + c) * 2 + (lax.axis_index("ctx") ^ y_rel)
    return flat * rows + p % rows


def column(v, rows):
    return jnp.pad(v, (0, rows - v.shape[0]))[:, None]


def shards(
    tokens, image_starts, attn_gain, query_weight, query_bias, key_weight, key_bias, value_weight, value_bias,
    out_weight, mlp_gain, gate_weight, up_weight, down_weight, cotangent,
):
    length, width = tokens.shape
    count = lax.axis_size("zz")
    devices = 8 * count
    rows = width // devices
    core = lax.axis_index("core")
    ctx = lax.axis_index("ctx")
    core_arr = core.reshape(1).astype(jnp.int32)
    feat = query_weight.shape[1]
    kv_feat = key_weight.shape[1]
    ff = gate_weight.shape[1]
    half_ff = ff // 2
    units = half_ff // LANES
    cuts = [0, units // 5 * 2 + 2, units]
    chunks = tuple((a * LANES, (b - a) * LANES) for a, b in zip(cuts, cuts[1:]))
    n = len(chunks)
    own_first = core == 0

    extras = jnp.concatenate(
        [column(v, rows) for v in (attn_gain, mlp_gain, query_bias, key_bias, value_bias)]
        + [jnp.zeros((rows, EXTRA - 5), BF16)], axis=1)
    fh, kh = feat // 2, kv_feat // 2
    a_own = pair_rows(*pack_attn(core_arr, query_weight, key_weight, value_weight, out_weight, extras))
    tokens, cotangent = after((tokens, cotangent), a_own)
    a_zs = along_z(a_own, True)
    gate_weight, up_weight, down_weight = after((gate_weight, up_weight, down_weight), a_own)
    packed = pack(core_arr, gate_weight, up_weight, down_weight, chunks)
    own = [pair_rows(packed[i], packed[n + i]) for i in range(n)]
    f_zs = [along_z(v, False) for v in own]

    natural = device_order(rows, count)
    to_dev = bf(jnp.arange(width, dtype=jnp.int32)[:, None] == natural[None, :])
    x = nn(tokens, to_dev)
    r1 = lax.rsqrt(jnp.mean(x * x, axis=-1, keepdims=True) + eps)
    table = rope_table(ctx * length, length)
    table_rem = rope_table((1 - ctx) * length, length)

    a_xs, a_ys = beside(a_zs)
    a_pieces = [a_zs, a_xs, a_ys, *diagonal(a_xs, a_ys)]
    w_mine = jnp.concatenate(a_pieces, axis=0)
    w_side = [w_mine, swap(w_mine, "core")]

    q0, k0, v0, o0, e0 = 0, fh, fh + kh, fh + 2 * kh, 2 * fh + 2 * kh
    extra_rel = w_mine[:, e0:]
    gains = jnp.transpose(f32(extra_rel[:, :2]))
    gain_attn, gain_mlp = gains[0:1], gains[1:2]
    bias_nat = nn(to_dev, extra_rel)
    q_bias = bias_nat[:, 2]
    kv_rows = kv_feat // devices
    k_bias = bias_nat[:, 3].reshape(devices, rows)[:, :kv_rows].reshape(-1)
    v_bias = bias_nat[:, 4].reshape(devices, rows)[:, :kv_rows].reshape(-1)

    def by_side(v):
        lo, hi = v[: v.shape[0] // 2], v[v.shape[0] // 2 :]
        return jnp.where(own_first, lo, hi), jnp.where(own_first, hi, lo)

    normed_one = bf(x * r1 * gain_attn)
    keys_values = []
    for w_all, kb, vb in zip(w_side, by_side(k_bias), by_side(v_bias)):
        kv = lax.dot_general(w_all[:, k0:o0], normed_one, (((0,), (1,)), ((), ())), preferred_element_type=F32)
        kv = kv + jnp.concatenate([kb, vb])[:, None]
        keys_values.append(jnp.concatenate([bf(rope(kv[:kh], table)), bf(kv[kh:])], axis=0))
    kv_rem = swap(jnp.concatenate(keys_values, axis=0), "ctx")
    kv_rem = [kv_rem[: 2 * kh], kv_rem[2 * kh :]]
    queries = []
    for w_all, qb in zip(w_side, by_side(q_bias)):
        q = lax.dot_general(w_all[:, :k0], after(normed_one, *keys_values), (((0,), (1,)), ((), ())), preferred_element_type=F32)
        queries.append(bf(rope(q + qb[:, None], table) * HD**-0.5))
    f_xy = [None] * n
    f_diag = [None] * n
    f_xs = swap(after(f_zs[0], normed_one), "xx")
    f_ys = swap(after(f_zs[0], *kv_rem), "ctx")
    f_xy[0] = (f_xs, f_ys)

    info = jnp.concatenate([ctx.reshape(1).astype(jnp.int32), image_starts[0]])
    bq = min(256, length)
    bk = min(256, length)
    queries[0] = after(queries[0], f_zs[0])
    att0, rest0, lse0 = attn_fwd(info, queries[0], keys_values[0], kv_rem[0], bq, bk)
    f_xy[0] = after(f_xy[0], att0)
    f_diag[0] = diagonal(*f_xy[0])
    f_zs[1] = after(f_zs[1], att0)
    f_xy[1] = beside(f_zs[1])
    queries[1] = after(queries[1], f_xy[0], f_zs[1])
    att1, rest1, lse1 = attn_fwd(info, queries[1], keys_values[1], kv_rem[1], bq, bk)
    f_xy[1] = after(f_xy[1], att1)
    f_diag[1] = diagonal(*f_xy[1])
    for i in range(2, n):
        f_zs[i] = after(f_zs[i], att1)
        f_xy[i] = beside(f_zs[i])
    attended, rest, lse = [att0, att1], [rest0, rest1], [lse0, lse1]

    cotangent = after(cotangent, att0)
    cot = bf(nn(cotangent, to_dev))
    cot_theirs = swap(cot, "core")
    hidden = x
    for a, w_all in zip(attended, w_side):
        hidden = hidden + lax.dot_general(a, w_all[:, o0:e0], (((0,), (1,)), ((), ())), preferred_element_type=F32)
    r2 = lax.rsqrt(jnp.mean(hidden * hidden, axis=-1, keepdims=True) + eps)
    normed_two = bf(hidden * r2 * gain_mlp)
    normed_theirs = swap(normed_two, "core")

    results, got_d, got_b, got_z = [], [None] * n, [None] * n, [None] * n
    x_in = normed_two
    for i in range(n):
        r = mlp(x_in, normed_theirs, cot, cot_theirs, [f_zs[i], *f_xy[i], *f_diag[i]])
        results.append(r)
        x_in = after(normed_two, r[2])
        if i + 2 < n:
            f_xy[i + 2] = after(f_xy[i + 2], r[2])
            f_diag[i + 2] = diagonal(*f_xy[i + 2])
        got_d[i] = sum_diagonal(r[4:])
        if i > 0:
            got_d[i - 1] = after(got_d[i - 1], r[2])
            got_b[i - 1] = sum_beside(results[i - 1][4:], got_d[i - 1])

    def total(a, b):
        mine = sum(f32(r[a]) for r in results)
        return mine + f32(swap(bf(sum(f32(r[b]) for r in results)), "core"))

    grad_two = total(2, 3)
    mlp_gain_grad = jnp.sum(grad_two * hidden * r2, axis=0)
    u = grad_two * gain_mlp
    grad_hidden = f32(cot) + r2 * u - hidden * (r2 * r2 * r2) * jnp.mean(u * hidden, axis=-1, keepdims=True)
    grad_attn = bf(grad_hidden)
    grad_mixed = [
        bf(lax.dot_general(w_all[:, o0:e0], grad_attn, (((0,), (1,)), ((), ())), preferred_element_type=F32)) for w_all in w_side
    ]

    back = [None, None]
    lows, kv_got = [], [None, None]
    for s in range(2):
        do = grad_mixed[s]
        if s == 1:
            zs = []
            for i in range(n - 1):
                zs.append(sum_own(results[i][4:], after(got_b[i], back[0][0])))
                got_z[i] = sum_along_z(zs[i], False)
            got_d[n - 1] = after(got_d[n - 1], back[0][0])
            got_b[n - 1] = sum_beside(results[n - 1][4:], got_d[n - 1])
            do = after(do, back[0][0], *zs)
        back[s] = attn_bwd(info, queries[s], do, attended[s], rest[s], lse[s], keys_values[s], kv_rem[s], table, table_rem, bq, bk)
        kv_got[s] = swap(back[s][2], "ctx")
    zs_last = sum_own(results[n - 1][4:], after(got_b[n - 1], back[1][0]))
    got_z[n - 1] = sum_along_z(zs_last, False)
    back[1] = after(back[1], zs_last)
    for s in range(2):
        query_low, d_loc, d_rem, _ = back[s]
        kv_low = bf(d_loc + f32(kv_got[s]))
        lows.append(jnp.concatenate([query_low, kv_low], axis=0))

    out_sum = total(0, 1)
    output = bf(nt(bf(hidden + out_sum), to_dev))
    mlp_out = [sum_pair(z) for z in got_z]
    gate_grad, up_grad, down_grad = unpack(core_arr, [m[0] for m in mlp_out], [m[1] for m in mlp_out], chunks, ff)

    out_grad = [lax.dot_general(grad_attn, a, (((0,), (1,)), ((), ())), preferred_element_type=F32) for a in attended]
    grad_one = 0.0
    for low, w_all in zip(lows, w_side):
        grad_one = grad_one + lax.dot_general(low, w_all[:, :o0], (((0,), (1,)), ((), ())), preferred_element_type=F32)
    w = grad_one * gain_attn
    tokens_grad_dev = grad_hidden + r1 * w - x * (r1 * r1 * r1) * jnp.mean(w * x, axis=-1, keepdims=True)
    tokens_grad = bf(nt(bf(tokens_grad_dev), to_dev))
    attn_gain_grad = jnp.sum(grad_one * x * r1, axis=0)
    qkv_grad = [lax.dot_general(normed_one, low, (((0,), (1,)), ((), ())), preferred_element_type=F32) for low in lows]
    bias_grad = [jnp.concatenate([jnp.sum(f32(b[0]), axis=1), jnp.sum(b[3], axis=1)]) for b in back]

    def whole_order(a, b):
        return jnp.where(own_first, jnp.concatenate([a, b]), jnp.concatenate([b, a]))

    def spread(v):
        return jnp.pad(v.reshape(devices, -1), ((0, 0), (0, rows - v.shape[0] // devices))).reshape(-1)

    qb, kb, vb = [whole_order(bias_grad[0][a:b], bias_grad[1][a:b]) for a, b in ((q0, k0), (k0, v0), (v0, o0))]
    nat_cols = jnp.stack([qb, spread(kb), spread(vb)], axis=0)
    dev_cols = nn(two_parts(nat_cols.T).T, to_dev)
    dev_cols = dev_cols[:3] + dev_cols[3:]
    vec_cols = jnp.concatenate([attn_gain_grad[None], mlp_gain_grad[None], dev_cols, jnp.zeros((EXTRA // 2 - 5, width), F32)], axis=0)
    extra_grad = two_parts(jnp.transpose(vec_cols))
    g_mine = jnp.concatenate([bf(qkv_grad[0]), bf(out_grad[0]), extra_grad], axis=1)
    g_theirs = jnp.concatenate([bf(qkv_grad[1]), bf(out_grad[1])], axis=1)
    got = swap(g_theirs, "core")
    g_sum = jnp.concatenate([bf(f32(g_mine[:, :e0]) + f32(got)), g_mine[:, e0:]], axis=1)
    quarter = width // 4
    bounds = [0, quarter, 2 * quarter, 3 * quarter, 3 * quarter + quarter // 2, width]
    g_pieces = [g_sum[a:b] for a, b in zip(bounds, bounds[1:])]
    g_got = sum_beside(g_pieces, sum_diagonal(g_pieces), EXTRA)
    a_mine, a_theirs = sum_pair(sum_along_z(sum_own(g_pieces, g_got, EXTRA), True))

    def natural_cols(a, b):
        lo, hi = a_mine[:, a:b], a_theirs[:, a:b]
        return jnp.where(own_first, jnp.concatenate([lo, hi], axis=1), jnp.concatenate([hi, lo], axis=1))

    extra = a_mine[:, e0:] + a_theirs[:, e0:]
    extra = extra[:, : EXTRA // 2] + extra[:, EXTRA // 2 :]
    return (
        output,
        tokens_grad,
        extra[:, 0],
        natural_cols(q0, k0),
        extra[:, 2],
        natural_cols(k0, v0),
        extra[:kv_rows, 3],
        natural_cols(v0, o0),
        extra[:kv_rows, 4],
        natural_cols(o0, e0),
        extra[:, 1],
        gate_grad,
        up_grad,
        down_grad,
    )


def solution(mesh):
    dp, ctx = mesh.devices.shape
    fine = Mesh(mesh.devices.reshape(dp // 4, 2, 2, ctx), ("zz", "xx", "core", "ctx"))
    every = ("zz", "xx", "core", "ctx")
    mat, vec = P(every, None), P(every)
    placed = (mat, P(("zz", "xx", "core"), None), vec, mat, vec, mat, vec, mat, vec, mat, vec, mat, mat, mat, mat)
    outs = (mat, mat, vec, mat, vec, mat, vec, mat, vec, mat, vec, mat, mat, mat)
    return jax.shard_map(shards, mesh=fine, in_specs=placed, out_specs=outs, check_vma=False)
```
